32 devices in a mesh: energy: 8 (over z, core), cell: 4 (over y, x).
Axes of the slice: x: 2, y: 2, z: 4, core: 2. Of those that a mesh axis runs over, the one named last changes fastest.
Arguments:
- green: bfloat16 [4, 48, 8, 16, 512], P(None, 'energy', 'cell'), may hold values from -6 to 6
- screened: bfloat16 [4, 48, 8, 16, 512], P(None, 'energy', None, 'cell'), may hold values from -6 to 6
- cell_map: int32 [8], replicated, may hold values from 0 to 7, each once
- shift_table: int32 [8, 8, 3], replicated, may hold values from 0 to 5, as said below
- shift_count: int32 [8, 8], replicated, may hold values from 1 to 3, as said below
Outputs:
- sigma: float32 [4, 48, 8, 16, 512], P(None, 'energy', 'cell')
The draws below stay inside these ranges and needn't reach their ends.
Inputs may be any that keep to these rules, and one draw needn't show every extreme that they name: `shift_table`: offsets of requested energies within the source group; slots c >= shift_count[g, s] are not read. `shift_count`: some destination group requests 3 energies from every source group. `cell_map`: each cell stands at exactly one position.
All inputs are finite; a program needn't handle non-finite values.
Results may differ from the reference program's by a relative error of at most 0.0003.
Values may be sent and summed in bfloat16 or wider, within the bound.
No kernel may reach another device: no remote copies, remote signals or barrier semaphores. Data moves between devices by JAX's collectives and lax.ppermute only.
A program may use at most 128 MiB of HBM per device.

```python
import jax
import jax.numpy as jnp
from jax import lax

B = 512
R = 16
E_DEV = 6
CAP = 3
NG = 8
NE = 48
NC = 8


def draw_shift_table(key, part):
    return jax.random.randint(key, (NG, NG, CAP), 0, E_DEV, dtype=jnp.int32)


def draw_shift_count(key, part):
    first_key, second_key = jax.random.split(key)
    base = jax.random.randint(first_key, (NG, NG), 1, CAP + 1, dtype=jnp.int32)
    full_row = jax.random.randint(second_key, (), 0, NG, dtype=jnp.int32)
    rows = lax.broadcasted_iota(jnp.int32, (NG, NG), 0)
    return jnp.where(rows == full_row, jnp.int32(CAP), base)


def block_levels(key, shape, shards, low, high):
    gain, own = 1.0, jax.random.fold_in(key, 6)
    for dim, parts in shards:
        steps = jnp.exp(jax.random.uniform(jax.random.fold_in(own, dim), (parts,), jnp.float32, low / len(shards), high / len(shards)))
        gain = gain * jnp.repeat(steps, shape[dim] // parts).reshape([-1 if axis == dim else 1 for axis in range(len(shape))])
    return gain


def bell_draw(stream_key, shape, width, most, cuts=(), held_as=jnp.bfloat16):
    result = jax.random.normal(stream_key, shape, jnp.float32) * width
    if len(cuts) > 0:
        result = block_levels(stream_key, shape, cuts, -0.22, 0.18) * result
    return jnp.clip(result, min=-most, max=most).astype(held_as)


def setup_inputs(seed: int = 0) -> dict:
    splits = jax.random.split(jax.random.key(seed), 6)
    green = bell_draw(splits[0], (4, NE, NC, R, B), 1.0, 6.0, ((1, 8), (2, 4)))
    screened = bell_draw(splits[1], (4, NE, NC, R, B), 1.0, 6.0, ((1, 8), (3, 4)))
    cell_map = jax.random.permutation(splits[2], NC).astype(jnp.int32)
    shift_table = draw_shift_table(jax.random.fold_in(splits[5], 71), 0)
    shift_count = draw_shift_count(jax.random.fold_in(splits[5], 71), 0)
    return {"green": green, "screened": screened, "cell_map": cell_map, "shift_table": shift_table, "shift_count": shift_count}


SCALE = 0.2


def complex_terms(windows, values):
    g_real = windows[:, 0::2]
    g_imag = windows[:, 1::2]
    w_real = values[:, 0::2]
    w_imag = values[:, 1::2]
    real_part = -(g_real * w_imag + g_imag * w_real)
    imag_part = g_real * w_real - g_imag * w_imag
    stacked = jnp.stack([real_part, imag_part], axis=2)
    return stacked.reshape((stacked.shape[0], 4) + stacked.shape[3:])


def reference(green, screened, cell_map, shift_table, shift_count):
    owned = jnp.take(screened, cell_map, axis=2)
    padding = jnp.zeros((4, E_DEV) + green.shape[2:], green.dtype)
    padded = jnp.concatenate([padding, green], axis=1)
    slots = jnp.arange(CAP, dtype=jnp.int32)

    def one_group(group):
        first = (group * E_DEV).astype(jnp.int32)
        table_row = shift_table[group]
        counts = shift_count[group]

        def turn(total, source):
            energies = (source * E_DEV + table_row[source]).astype(jnp.int32)
            live = (slots < counts[source]).astype(jnp.float32)
            starts = (jnp.maximum(first - energies, -E_DEV) + E_DEV).astype(jnp.int32)
            windows = jax.vmap(lambda begin: lax.dynamic_slice_in_dim(padded, begin, E_DEV, 1))(starts)
            values = jnp.moveaxis(jnp.take(owned, energies, axis=1), 1, 0)
            terms = complex_terms(windows.astype(jnp.float32), values.astype(jnp.float32)[:, :, None])
            return total + jnp.sum(terms * live[:, None, None, None, None, None], axis=0), None

        zeros = jnp.zeros((4, E_DEV, NC, R, B), jnp.float32)
        total, _ = lax.scan(turn, zeros, jnp.arange(NG, dtype=jnp.int32))
        return total * SCALE

    blocks = lax.map(one_group, jnp.arange(NG, dtype=jnp.int32))
    return jnp.moveaxis(blocks, 0, 1).reshape(4, NE, NC, R, B)
```

```python
import functools

import jax
import jax.numpy as jnp
from jax import lax
from jax.experimental import pallas as pl
from jax.experimental.pallas import tpu as pltpu
from jax.sharding import PartitionSpec as P

SCALE = 0.2
LANES = 128


def slice_of(index, tiles, parts):
    return index // (tiles * parts), (index // parts) % tiles, index % parts


def pack_kernel(groups, tiles, parts, me_ref, whole_ref, *refs):
    outs, sems = refs[:groups], refs[groups]
    me = me_ref[0]
    rows = outs[0].shape[2]
    copies = []
    for k in range(groups):
        cell, tile, part = slice_of(me ^ k, tiles, parts)
        source = whole_ref.at[:, :, cell, pl.ds(part * rows, rows), pl.ds(pl.multiple_of(tile * LANES, LANES), LANES)]
        copies.append(pltpu.make_async_copy(source, outs[k], sems.at[k]))
    for copy in copies:
        copy.start()
    for copy in copies:
        copy.wait()


def pack(me, whole, groups, tiles, parts):
    comps, energies, _, rows, _ = whole.shape
    block = jax.ShapeDtypeStruct((comps, energies, rows // parts, LANES), whole.dtype)
    return pl.pallas_call(
        functools.partial(pack_kernel, groups, tiles, parts),
        out_shape=[block] * groups,
        in_specs=[pl.BlockSpec(memory_space=pltpu.SMEM), pl.BlockSpec(memory_space=pl.ANY)],
        out_specs=[pl.BlockSpec(memory_space=pl.ANY)] * groups,
        scratch_shapes=[pltpu.SemaphoreType.DMA((groups,))],
        name="pack",
    )(me, whole)


def sigma_kernel(groups, per_energy, slots, me_ref, table_ref, count_ref, *refs):
    greens, screens = refs[:groups], refs[groups : 2 * groups]
    outs = refs[2 * groups : 3 * groups]
    g_all, w_all = refs[3 * groups :]
    me = me_ref[0]
    plane = g_all.shape[2:]
    for comp in range(4):
        for j in range(per_energy):
            g_all[comp, j] = jnp.zeros(plane, jnp.float32)
    for k in range(groups):
        source = me ^ k
        for comp in range(4):
            for j in range(per_energy):
                g_all[comp, (source + 1) * per_energy + j] = greens[k][comp, j].astype(jnp.float32)
                w_all[comp, source * per_energy + j] = screens[k][comp, j].astype(jnp.float32)
    for k in range(groups):
        group = me ^ k
        for kind in range(2):

            def turn(source, sums):
                sums = list(sums)
                count = count_ref[group, source]
                for slot in range(slots):
                    shift = jnp.clip(table_ref[group * groups + source, slot], 0, per_energy - 1)
                    live = jnp.where(slot < count, 1.0, 0.0).astype(jnp.float32)
                    energy = source * per_energy + shift
                    start = (group - source + 1) * per_energy - shift
                    w_real = w_all[2 * kind, energy] * live
                    w_imag = w_all[2 * kind + 1, energy] * live
                    for j in range(per_energy):
                        g_real = g_all[2 * kind, start + j]
                        g_imag = g_all[2 * kind + 1, start + j]
                        sums[2 * j] = sums[2 * j] - (g_real * w_imag + g_imag * w_real)
                        sums[2 * j + 1] = sums[2 * j + 1] + (g_real * w_real - g_imag * w_imag)
                return tuple(sums)

            zeros = tuple(jnp.zeros(plane, jnp.float32) for _ in range(2 * per_energy))
            sums = lax.fori_loop(0, group + 1, turn, zeros)
            for j in range(per_energy):
                outs[k][2 * kind, j] = sums[2 * j] * SCALE
                outs[k][2 * kind + 1, j] = sums[2 * j + 1] * SCALE


def compute(me, table, count, greens, screens):
    groups = len(greens)
    comps, per_energy, rows, lanes = greens[0].shape
    slots = table.shape[-1]
    smem, vmem = pl.BlockSpec(memory_space=pltpu.SMEM), pl.BlockSpec(memory_space=pltpu.VMEM)
    return pl.pallas_call(
        functools.partial(sigma_kernel, groups, per_energy, slots),
        out_shape=[jax.ShapeDtypeStruct(greens[0].shape, jnp.float32)] * groups,
        in_specs=[smem] * 3 + [vmem] * (2 * groups),
        out_specs=[vmem] * groups,
        scratch_shapes=[
            pltpu.VMEM((comps, (groups + 1) * per_energy, rows, lanes), jnp.float32),
            pltpu.VMEM((comps, groups * per_energy, rows, lanes), jnp.float32),
        ],
        compiler_params=pltpu.CompilerParams(vmem_limit_bytes=48 * 1024 * 1024),
        name="sigma",
    )(me, table.reshape(groups * groups, slots), count, *greens, *screens)


def unpack_kernel(groups, tiles, parts, me_ref, *refs):
    blocks, whole_ref, sems = refs[:groups], refs[groups], refs[groups + 1]
    me = me_ref[0]
    rows = blocks[0].shape[2]
    copies = []
    for k in range(groups):
        cell, tile, part = slice_of(me ^ k, tiles, parts)
        target = whole_ref.at[:, :, cell, pl.ds(part * rows, rows), pl.ds(pl.multiple_of(tile * LANES, LANES), LANES)]
        copies.append(pltpu.make_async_copy(blocks[k], target, sems.at[k]))
    for copy in copies:
        copy.start()
    for copy in copies:
        copy.wait()


def unpack(me, blocks, shape, tiles, parts):
    groups = len(blocks)
    return pl.pallas_call(
        functools.partial(unpack_kernel, groups, tiles, parts),
        out_shape=jax.ShapeDtypeStruct(shape, blocks[0].dtype),
        in_specs=[pl.BlockSpec(memory_space=pltpu.SMEM)] + [pl.BlockSpec(memory_space=pl.ANY)] * groups,
        out_specs=pl.BlockSpec(memory_space=pl.ANY),
        scratch_shapes=[pltpu.SemaphoreType.DMA((groups,))],
        name="unpack",
    )(me, *blocks)


def exchange(blocks):
    groups = len(blocks)
    got = list(blocks)
    middle = list(range(groups // 2, groups)) + list(range(1, groups // 2))
    for k in middle:
        got[k] = lax.ppermute(blocks[k], "energy", [(i, i ^ k) for i in range(groups)])
    return got


def per_device(green, screened, cell_map, shift_table, shift_count):
    groups = lax.axis_size("energy")
    cell_count = lax.axis_size("cell")
    per_energy, per_cell, rows, width = green.shape[1:]
    tiles = width // LANES
    parts = groups // (per_cell * tiles)
    me = lax.axis_index("energy").astype(jnp.int32).reshape(1)

    greens = exchange(pack(me, green, groups, tiles, parts))

    wanted = jnp.transpose(cell_map.reshape(cell_count, per_cell)).reshape(-1)
    outgoing = jnp.take(screened, wanted, axis=2)
    outgoing = outgoing.reshape(4, per_energy, per_cell, cell_count, screened.shape[3], width)
    arrived = lax.all_to_all(outgoing, "cell", split_axis=3, concat_axis=3, tiled=True)
    owned = arrived.reshape(4, per_energy, per_cell, rows, width)
    screens = exchange(pack(me, owned, groups, tiles, parts))

    sums = compute(me, shift_table, shift_count, greens, screens)
    return unpack(me, exchange(sums), green.shape, tiles, parts)


def solution(mesh):
    placed = (
        P(None, "energy", "cell", None, None),
        P(None, "energy", None, "cell", None),
        P(),
        P(),
        P(),
    )
    return jax.shard_map(
        per_device,
        mesh=mesh,
        in_specs=placed,
        out_specs=P(None, "energy", "cell", None, None),
        check_vma=False,
    )
```

```python
import functools

import jax
import jax.numpy as jnp
from jax import lax
from jax.experimental import pallas as pl
from jax.experimental.pallas import tpu as pltpu
from jax.sharding import PartitionSpec as P

SCALE = 0.2
LANES = 128
PAIR = 2
STEPS = 32700.0
FINE = 64.0
TINY = 1e-34
SMEM = pl.BlockSpec(memory_space=pltpu.SMEM)
VMEM = pl.BlockSpec(memory_space=pltpu.VMEM)
ANY = pl.BlockSpec(memory_space=pl.ANY)
PARAMS = pltpu.CompilerParams(vmem_limit_bytes=48 * 1024 * 1024)


def slice_of(index, tiles, parts):
    return index // (tiles * parts), (index // parts) % tiles, index % parts


def lanes_of(tile):
    return pl.ds(pl.multiple_of(tile * LANES, LANES), LANES)


def pack_kernel(groups, cells, tiles, parts, me_ref, map_ref, green_ref, screened_ref, *outs):
    me, column = me_ref[0], me_ref[1]
    comps, energies, rows, _ = outs[0].shape
    for k in range(groups):
        cell, tile, part = slice_of(me ^ k, tiles, parts)
        for comp in range(comps):
            for j in range(energies):
                if parts == 1:
                    outs[k][comp, j] = green_ref[comp, j, cell, :, lanes_of(tile)]
                else:
                    block = green_ref[comp, j, cell, :, lanes_of(tile)].astype(jnp.float32)
                    chosen = block[:rows]
                    for other in range(1, parts):
                        chosen = jnp.where(part == other, block[other * rows : (other + 1) * rows], chosen)
                    outs[k][comp, j] = chosen.astype(outs[k].dtype)
    per_cell = green_ref.shape[2]
    for k in range(cells):
        for q in range(per_cell):
            cell = map_ref[(column ^ k) * per_cell + q]
            for comp in range(comps):
                for j in range(energies):
                    outs[groups + k][comp, j, q] = screened_ref[comp, j, cell]


def pack(me, cell_map, green, screened, groups, cells, tiles, parts):
    comps, energies, per_cell, rows, width = green.shape
    block = jax.ShapeDtypeStruct((comps, energies, rows // parts, LANES), green.dtype)
    quarter = jax.ShapeDtypeStruct((comps, energies, per_cell, screened.shape[3], width), screened.dtype)
    outs = pl.pallas_call(
        functools.partial(pack_kernel, groups, cells, tiles, parts),
        out_shape=[block] * groups + [quarter] * cells,
        in_specs=[SMEM, SMEM, VMEM, VMEM],
        out_specs=[VMEM] * (groups + cells),
        compiler_params=PARAMS,
        name="pack",
    )(me, cell_map, green, screened)
    return outs[:groups], outs[groups:]


def place_kernel(groups, cells, tiles, parts, me_ref, *refs):
    quarters, outs = refs[:cells], refs[cells : cells + groups]
    held, whole, sems = refs[cells + groups :]
    me, column = me_ref[0], me_ref[1]
    comps, energies, rows, _ = outs[0].shape
    per_cell, depth = quarters[0].shape[2:4]
    copies = [pltpu.make_async_copy(quarters[k], held.at[column ^ k], sems.at[k]) for k in range(cells)]
    for copy in copies:
        copy.start()
    for copy in copies:
        copy.wait()
    for comp in range(comps):
        for j in range(energies):
            for q in range(per_cell):
                for c in range(cells):
                    whole[comp, j, q, c * depth : (c + 1) * depth, :] = held[c, comp, j, q].astype(jnp.float32)
    for k in range(groups):
        cell, tile, part = slice_of(me ^ k, tiles, parts)
        place = slice(None) if parts == 1 else pl.ds(pl.multiple_of(part * rows, rows), rows)
        for comp in range(comps):
            for j in range(energies):
                outs[k][comp, j] = whole[comp, j, cell, place, lanes_of(tile)].astype(outs[k].dtype)


def place(me, quarters, groups, tiles, parts):
    cells = len(quarters)
    comps, energies, per_cell, depth, width = quarters[0].shape
    block = jax.ShapeDtypeStruct((comps, energies, cells * depth // parts, LANES), quarters[0].dtype)
    return pl.pallas_call(
        functools.partial(place_kernel, groups, cells, tiles, parts),
        out_shape=[block] * groups,
        in_specs=[SMEM] + [ANY] * cells,
        out_specs=[VMEM] * groups,
        scratch_shapes=[
            pltpu.VMEM((cells,) + quarters[0].shape, quarters[0].dtype),
            pltpu.VMEM((comps, energies, per_cell, cells * depth, width), jnp.float32),
            pltpu.SemaphoreType.DMA((cells,)),
        ],
        compiler_params=PARAMS,
        name="place",
    )(me, *quarters)


def scale_rows(per_energy, comps):
    return comps * (per_energy // PAIR)


def sigma_kernel(groups, per_energy, slots, ks, me_ref, table_ref, count_ref, *refs):
    greens, screens = refs[:groups], refs[groups : 2 * groups]
    outs = refs[2 * groups : 2 * groups + len(ks)]
    g_held, w_all, g_all, sems = refs[2 * groups + len(ks) :]
    me = me_ref[0]
    plane = g_all.shape[2:]
    copies = []
    for k in range(groups):
        copies.append(pltpu.make_async_copy(greens[k], g_held.at[me ^ k], sems.at[0, k]))
        copies.append(pltpu.make_async_copy(screens[k], w_all.at[me ^ k], sems.at[1, k]))
    for copy in copies:
        copy.start()
    for copy in copies:
        copy.wait()
    for comp in range(4):
        for j in range(per_energy):
            g_all[comp, j] = jnp.zeros(plane, jnp.float32)
            for source in range(groups):
                g_all[comp, (source + 1) * per_energy + j] = g_held[source, comp, j].astype(jnp.float32)
    row = lax.broadcasted_iota(jnp.int32, plane, 0)
    for at, k in enumerate(ks):
        group = me ^ k
        scale_planes = -(-scale_rows(per_energy, 4) // plane[0])
        codes = [jnp.zeros(plane, jnp.float32) for _ in range(scale_planes)]
        for kind in range(2):

            def turn(source, sums):
                sums = list(sums)
                count = count_ref[group, source]
                for slot in range(slots):
                    shift = jnp.clip(table_ref[group * groups + source, slot], 0, per_energy - 1)
                    live = jnp.where(slot < count, 1.0, 0.0).astype(jnp.float32)
                    start = (group - source + 1) * per_energy - shift
                    w_real = w_all[source, 2 * kind, shift].astype(jnp.float32) * live
                    w_imag = w_all[source, 2 * kind + 1, shift].astype(jnp.float32) * live
                    for j in range(per_energy):
                        g_real = g_all[2 * kind, start + j]
                        g_imag = g_all[2 * kind + 1, start + j]
                        sums[j] = sums[j] - (g_real * w_imag + g_imag * w_real)
                        sums[per_energy + j] = sums[per_energy + j] + (g_real * w_real - g_imag * w_imag)
                return tuple(sums)

            zeros = tuple(jnp.zeros(plane, jnp.float32) for _ in range(2 * per_energy))
            sums = lax.fori_loop(0, group + 1, turn, zeros)
            sums = [total * SCALE for total in sums]
            if k == 0:
                for part in range(2):
                    for j in range(per_energy):
                        outs[at][2 * kind + part, j] = sums[part * per_energy + j]
                continue
            for first in range(0, 2 * per_energy, PAIR):
                pair = sums[first : first + PAIR]
                largest = functools.reduce(jnp.maximum, [jnp.abs(total) for total in pair])
                largest = jnp.maximum(jnp.max(largest, axis=0, keepdims=True), TINY)
                code = jnp.ceil(jnp.log2(largest) * FINE)
                inverse = jnp.exp2(code * (-1.0 / FINE)) * STEPS
                where = (kind * 2 * per_energy + first) // PAIR
                codes[where // plane[0]] = jnp.where(row == where % plane[0], code, codes[where // plane[0]])
                for j, total in enumerate(pair):
                    coded = jnp.round(total * inverse).astype(jnp.int32)
                    outs[at][kind * 2 * per_energy + first + j] = coded.astype(jnp.int16)
        if k != 0:
            for j in range(scale_planes):
                outs[at][4 * per_energy + j] = codes[j].astype(jnp.int32).astype(jnp.int16)


def sigma_of(me, table, count, greens, screens, ks):
    groups = len(greens)
    comps, per_energy, rows, lanes = greens[0].shape
    slots = table.shape[-1]
    planes = comps * per_energy + -(-scale_rows(per_energy, comps) // rows)
    own = jax.ShapeDtypeStruct(greens[0].shape, jnp.float32)
    coded = jax.ShapeDtypeStruct((planes, rows, lanes), jnp.int16)
    return pl.pallas_call(
        functools.partial(sigma_kernel, groups, per_energy, slots, ks),
        out_shape=[own if k == 0 else coded for k in ks],
        in_specs=[SMEM] * 3 + [ANY] * (2 * groups),
        out_specs=[VMEM] * len(ks),
        scratch_shapes=[
            pltpu.VMEM((groups,) + greens[0].shape, greens[0].dtype),
            pltpu.VMEM((groups,) + greens[0].shape, greens[0].dtype),
            pltpu.VMEM((comps, (groups + 1) * per_energy, rows, lanes), jnp.float32),
            pltpu.SemaphoreType.DMA((2, groups)),
        ],
        compiler_params=PARAMS,
        name="sigma",
    )(me, table.reshape(groups * groups, slots), count, *greens, *screens)


def unpack_kernel(groups, tiles, parts, me_ref, *refs):
    blocks, whole_ref = refs[:groups], refs[groups]
    me = me_ref[0]
    comps, energies, rows, _ = blocks[0].shape
    for k in range(groups):
        cell, tile, part = slice_of(me ^ k, tiles, parts)
        spot = slice(None) if parts == 1 else pl.ds(pl.multiple_of(part * rows, rows), rows)
        scales = []
        if k != 0:
            for j in range(blocks[k].shape[0] - comps * energies):
                code = blocks[k][comps * energies + j].astype(jnp.int32).astype(jnp.float32)
                scales.append(jnp.exp2(code * (1.0 / FINE)) * (1.0 / STEPS))
        for comp in range(comps):
            for j in range(energies):
                if k == 0:
                    value = blocks[0][comp, j]
                else:
                    where = (comp * energies + j) // PAIR
                    scale = scales[where // rows][where % rows : where % rows + 1]
                    value = blocks[k][comp * energies + j].astype(jnp.int32).astype(jnp.float32) * scale
                whole_ref[comp, j, cell, spot, lanes_of(tile)] = value


def unpack(me, blocks, shape, tiles, parts):
    groups = len(blocks)
    return pl.pallas_call(
        functools.partial(unpack_kernel, groups, tiles, parts),
        out_shape=jax.ShapeDtypeStruct(shape, jnp.float32),
        in_specs=[SMEM] + [VMEM] * groups,
        out_specs=VMEM,
        compiler_params=PARAMS,
        name="unpack",
    )(me, *blocks)


def swap(block, axis, count, k):
    return block if k == 0 else lax.ppermute(block, axis, [(i, i ^ k) for i in range(count)])


def per_device(green, screened, cell_map, shift_table, shift_count):
    groups = lax.axis_size("energy")
    cells = lax.axis_size("cell")
    per_energy, per_cell, rows, width = green.shape[1:]
    tiles = width // LANES
    parts = groups // (per_cell * tiles)
    me = jnp.stack([lax.axis_index("energy"), lax.axis_index("cell")]).astype(jnp.int32)
    far = list(range(groups // 2, groups))
    near = list(range(groups // 2))

    greens, quarters = pack(me, cell_map, green, screened, groups, cells, tiles, parts)
    greens = {k: swap(greens[k], "energy", groups, k) for k in far + near}
    quarters = [swap(quarters[k], "cell", cells, k) for k in range(cells)]
    screens = place(me, quarters, groups, tiles, parts)
    screens = {k: swap(screens[k], "energy", groups, k) for k in far + near}
    every = range(groups)
    parts_in = ([greens[k] for k in every], [screens[k] for k in every])
    sums = {}
    for ks in (far, near):
        for k, block in zip(ks, sigma_of(me, shift_table, shift_count, *parts_in, ks)):
            sums[k] = swap(block, "energy", groups, k)
    return unpack(me, [sums[k] for k in every], green.shape, tiles, parts)


def solution(mesh):
    placed = (
        P(None, "energy", "cell", None, None),
        P(None, "energy", None, "cell", None),
        P(),
        P(),
        P(),
    )
    return jax.shard_map(
        per_device,
        mesh=mesh,
        in_specs=placed,
        out_specs=P(None, "energy", "cell", None, None),
        check_vma=False,
    )
```

```python
import functools

import jax
import jax.numpy as jnp
from jax import lax
from jax.experimental import pallas as pl
from jax.experimental.pallas import tpu as pltpu
from jax.sharding import PartitionSpec as P

SCALE = 0.2
LANES = 128
PAIR = 2
STEPS = 32700.0
FINE = 64.0
TINY = 1e-34
SMEM = pl.BlockSpec(memory_space=pltpu.SMEM)
VMEM = pl.BlockSpec(memory_space=pltpu.VMEM)
HBM = pl.BlockSpec(memory_space=pltpu.HBM)
PARAMS = pltpu.CompilerParams(vmem_limit_bytes=32 * 1024 * 1024)


class Sizes:
    def __init__(self, green, screened, groups, cells):
        self.comps, self.energies, self.per_cell, self.rows, self.width = green.shape
        self.groups, self.cells = groups, cells
        self.tiles = self.width // LANES
        self.slices = groups // self.per_cell
        self.parts = self.slices // self.tiles
        self.held = screened.shape[3]
        self.plane = (self.rows // self.parts, LANES)
        self.planes = self.comps * self.energies
        self.scales = self.planes // PAIR
        self.scale_planes = -(-self.scales // self.plane[0])

    def where(self, index):
        cell, tile, part = index // self.slices, (index // self.parts) % self.tiles, index % self.parts
        return cell, part, pl.ds(pl.multiple_of(tile * LANES, LANES), LANES)


def part_of(s, value, part):
    count = value.shape[0] // s.parts
    chosen = value[:count]
    for other in range(1, s.parts):
        chosen = jnp.where(part == other, value[other * count : (other + 1) * count], chosen)
    return chosen


def pick_kernel(s, map_ref, screened_ref, out_ref):
    for column in range(s.cells):
        for q in range(s.per_cell):
            cell = map_ref[column * s.per_cell + q]
            for t in range(s.tiles):
                target = (q * s.slices + t) * s.cells + column
                for comp in range(s.comps):
                    for j in range(s.energies):
                        part = screened_ref[comp, j, cell, :, t * LANES : (t + 1) * LANES]
                        out_ref[target, comp * s.energies + j] = part


def pick_screened(s, cell_map, screened):
    shape = (s.groups * s.cells, s.planes, s.held, LANES)
    return pl.pallas_call(
        functools.partial(pick_kernel, s),
        out_shape=jax.ShapeDtypeStruct(shape, screened.dtype),
        in_specs=[SMEM, VMEM],
        out_specs=VMEM,
        compiler_params=PARAMS,
        name="pick_screened",
    )(cell_map, screened)


def cut_kernel(s, me_ref, green_ref, *greens):
    me = me_ref[0]
    for k in range(s.groups):
        cell, part, lanes = s.where(me ^ k)
        for comp in range(s.comps):
            for j in range(s.energies):
                if s.parts == 1:
                    greens[k][comp * s.energies + j] = green_ref[comp, j, cell, :, lanes]
                else:
                    value = green_ref[comp, j, cell, :, lanes].astype(jnp.float32)
                    greens[k][comp * s.energies + j] = part_of(s, value, part).astype(greens[k].dtype)


def cut_green(s, me, green):
    return pl.pallas_call(
        functools.partial(cut_kernel, s),
        out_shape=[jax.ShapeDtypeStruct((s.planes,) + s.plane, green.dtype)] * s.groups,
        in_specs=[SMEM, VMEM],
        out_specs=[VMEM] * s.groups,
        compiler_params=PARAMS,
        name="cut_green",
    )(me, green)


def stage_kernel(s, me_ref, screens_ref, *refs):
    greens = refs[: s.groups]
    g_all, w_all = refs[s.groups :]
    me = me_ref[0]
    zero = jnp.zeros(s.plane, jnp.float32)
    for comp in range(s.comps):
        for j in range(s.energies):
            plane = comp * s.energies + j
            g_all[comp, j] = zero
            for k in range(s.groups):
                g_all[comp, ((me ^ k) + 1) * s.energies + j] = greens[k][plane].astype(jnp.float32)
            for source in range(s.groups):
                if s.parts > 1:
                    w_all[source, comp, j] = screens_ref[source, plane].astype(jnp.float32)
                    continue
                for c in range(s.cells):
                    piece = screens_ref[source * s.cells + c, plane].astype(jnp.float32)
                    w_all[source, comp, j, c * s.held : (c + 1) * s.held, :] = piece


def stage(s, me, greens, screens):
    return pl.pallas_call(
        functools.partial(stage_kernel, s),
        out_shape=[
            jax.ShapeDtypeStruct((s.comps, (s.groups + 1) * s.energies) + s.plane, jnp.float32),
            jax.ShapeDtypeStruct((s.groups, s.comps, s.energies) + s.plane, jnp.float32),
        ],
        in_specs=[SMEM] + [VMEM] * (s.groups + 1),
        out_specs=[VMEM] * 2,
        compiler_params=PARAMS,
        name="stage",
    )(me, screens, *greens)


def sigma_kernel(s, slots, ks, me_ref, table_ref, count_ref, g_all, w_all, *outs):
    me = me_ref[0]
    row = lax.broadcasted_iota(jnp.int32, s.plane, 0)
    for at, k in enumerate(ks):
        group = me ^ k
        codes = [jnp.zeros(s.plane, jnp.float32) for _ in range(s.scale_planes)]
        for kind in range(2):

            def turn(source, sums):
                sums = list(sums)
                count = count_ref[group, source]
                for slot in range(slots):
                    shift = jnp.clip(table_ref[group * s.groups + source, slot], 0, s.energies - 1)
                    live = jnp.where(slot < count, 1.0, 0.0).astype(jnp.float32)
                    start = (group - source + 1) * s.energies - shift
                    w_real = w_all[source, 2 * kind, shift] * live
                    w_imag = w_all[source, 2 * kind + 1, shift] * live
                    for j in range(s.energies):
                        g_real = g_all[2 * kind, start + j]
                        g_imag = g_all[2 * kind + 1, start + j]
                        sums[j] = sums[j] - (g_real * w_imag + g_imag * w_real)
                        sums[s.energies + j] = sums[s.energies + j] + (g_real * w_real - g_imag * w_imag)
                return tuple(sums)

            zeros = tuple(jnp.zeros(s.plane, jnp.float32) for _ in range(2 * s.energies))
            sums = lax.fori_loop(0, group + 1, turn, zeros)
            sums = [total * SCALE for total in sums]
            first = kind * 2 * s.energies
            if k == 0:
                for j, total in enumerate(sums):
                    outs[at][first + j] = total
                continue
            for low in range(0, 2 * s.energies, PAIR):
                pair = sums[low : low + PAIR]
                largest = functools.reduce(jnp.maximum, [jnp.abs(total) for total in pair])
                largest = jnp.maximum(jnp.max(largest, axis=0, keepdims=True), TINY)
                code = jnp.ceil(jnp.log2(largest) * FINE)
                inverse = jnp.exp2(code * (-1.0 / FINE)) * STEPS
                where = (first + low) // PAIR
                spot = where // s.plane[0]
                codes[spot] = jnp.where(row == where % s.plane[0], code, codes[spot])
                for j, total in enumerate(pair):
                    coded = jnp.round(total * inverse).astype(jnp.int32)
                    outs[at][first + low + j] = coded.astype(jnp.int16)
        if k != 0:
            for j in range(s.scale_planes):
                outs[at][s.comps * s.energies + j] = codes[j].astype(jnp.int32).astype(jnp.int16)


def sigma_of(s, me, table, count, g_all, w_all, ks):
    slots = table.shape[-1]
    planes = s.comps * s.energies
    own = jax.ShapeDtypeStruct((planes,) + s.plane, jnp.float32)
    coded = jax.ShapeDtypeStruct((planes + s.scale_planes,) + s.plane, jnp.int16)
    return pl.pallas_call(
        functools.partial(sigma_kernel, s, slots, ks),
        out_shape=[own if k == 0 else coded for k in ks],
        in_specs=[SMEM] * 3 + [VMEM] * 2,
        out_specs=[VMEM] * len(ks),
        compiler_params=PARAMS,
        name="sigma",
    )(me, table.reshape(s.groups * s.groups, slots), count, g_all, w_all)


def unpack_kernel(s, me_ref, *refs):
    blocks, whole_ref = refs[: s.groups], refs[s.groups]
    me = me_ref[0]
    for k, block in enumerate(blocks):
        cell, part, lanes = s.where(me ^ k)
        rows = slice(None) if s.parts == 1 else pl.ds(pl.multiple_of(part * s.plane[0], s.plane[0]), s.plane[0])
        scales = []
        if k != 0:
            for j in range(s.scale_planes):
                code = block[s.planes + j].astype(jnp.int32).astype(jnp.float32)
                scales.append(jnp.exp2(code * (1.0 / FINE)) * (1.0 / STEPS))
        for comp in range(s.comps):
            for j in range(s.energies):
                plane = comp * s.energies + j
                value = block[plane]
                if k != 0:
                    where = plane // PAIR
                    scale = scales[where // s.plane[0]][where % s.plane[0] : where % s.plane[0] + 1]
                    value = value.astype(jnp.int32).astype(jnp.float32) * scale
                whole_ref[comp, j, cell, rows, lanes] = value


def unpack(s, me, blocks):
    return pl.pallas_call(
        functools.partial(unpack_kernel, s),
        out_shape=jax.ShapeDtypeStruct((s.comps, s.energies, s.per_cell, s.rows, s.width), jnp.float32),
        in_specs=[SMEM] + [VMEM] * s.groups,
        out_specs=VMEM,
        compiler_params=PARAMS,
        name="unpack",
    )(me, *blocks)


def swap(s, block, k):
    return block if k == 0 else lax.ppermute(block, "energy", [(i, i ^ k) for i in range(s.groups)])


def send_screened(s, cell_map, screened):
    if s.parts == 1:
        return lax.all_to_all(pick_screened(s, cell_map, screened), ("energy", "cell"), 0, 0, tiled=True)
    chosen = jnp.take(screened, cell_map, axis=2).reshape(s.planes, s.cells, s.per_cell, s.held, s.width)
    whole = lax.all_to_all(chosen, "cell", 1, 3, tiled=True)
    cut = whole.reshape(s.planes, s.per_cell, s.parts, s.plane[0], s.tiles, LANES)
    cut = jnp.transpose(cut, (1, 4, 2, 0, 3, 5)).reshape((s.groups, s.planes) + s.plane)
    return lax.all_to_all(cut, "energy", 0, 0, tiled=True)


def per_device(green, screened, cell_map, shift_table, shift_count):
    s = Sizes(green, screened, lax.axis_size("energy"), lax.axis_size("cell"))
    me = jnp.stack([lax.axis_index("energy"), lax.axis_index("cell")]).astype(jnp.int32)
    half = s.groups // 2
    far, near = list(range(half, s.groups)), list(range(half))

    screens = send_screened(s, cell_map, screened)
    greens = [swap(s, block, k) for k, block in enumerate(cut_green(s, me, green))]
    g_all, w_all = stage(s, me, greens, screens)
    sums = {}
    for ks in (far, near):
        for k, block in zip(ks, sigma_of(s, me, shift_table, shift_count, g_all, w_all, ks)):
            sums[k] = swap(s, block, k)
    return unpack(s, me, [sums[k] for k in range(s.groups)])


def solution(mesh):
    placed = (
        P(None, "energy", "cell", None, None),
        P(None, "energy", None, "cell", None),
        P(),
        P(),
        P(),
    )
    return jax.shard_map(
        per_device,
        mesh=mesh,
        in_specs=placed,
        out_specs=P(None, "energy", "cell", None, None),
        check_vma=False,
    )
```

```python
import functools

import jax
import jax.numpy as jnp
from jax import lax
from jax.experimental import pallas as pl
from jax.experimental.pallas import tpu as pltpu
from jax.sharding import PartitionSpec as P

SCALE = 0.2
LANES = 128
PAIR = 2
halfS = 32700.0
FINE = 64.0
TINY = 1e-34
SMEM = pl.BlockSpec(memory_space=pltpu.SMEM)
VMEM = pl.BlockSpec(memory_space=pltpu.VMEM)
ANY = pl.BlockSpec(memory_space=pl.ANY)
PARAMS = pltpu.CompilerParams(vmem_limit_bytes=32 * 1024 * 1024)


class Sizes:
    def __init__(self, green, screened, groups, cells):
        self.comps, self.energies, self.per_cell, self.rows, self.width = green.shape
        self.groups, self.cells = groups, cells
        self.tiles = self.width // LANES
        self.slices = groups // self.per_cell
        self.parts = self.slices // self.tiles
        self.held = screened.shape[3]
        self.plane = (self.rows // self.parts, LANES)
        self.planes = self.comps * self.energies
        self.scales = self.planes // PAIR
        self.scale_planes = -(-self.scales // self.plane[0])

    def where(self, index):
        cell, tile, part = index // self.slices, (index // self.parts) % self.tiles, index % self.parts
        return cell, part, pl.ds(pl.multiple_of(tile * LANES, LANES), LANES)


def part_of(s, value, part):
    count = value.shape[0] // s.parts
    chosen = value[:count]
    for other in range(1, s.parts):
        chosen = jnp.where(part == other, value[other * count : (other + 1) * count], chosen)
    return chosen


def pick_kernel(s, map_ref, screened_ref, out_ref):
    for column in range(s.cells):
        for q in range(s.per_cell):
            cell = map_ref[column * s.per_cell + q]
            for t in range(s.tiles):
                target = (q * s.slices + t) * s.cells + column
                for comp in range(s.comps):
                    for j in range(s.energies):
                        part = screened_ref[comp, j, cell, :, t * LANES : (t + 1) * LANES]
                        out_ref[target, comp * s.energies + j] = part


def pick_screened(s, cell_map, screened):
    shape = (s.groups * s.cells, s.planes, s.held, LANES)
    return pl.pallas_call(
        functools.partial(pick_kernel, s),
        out_shape=jax.ShapeDtypeStruct(shape, screened.dtype),
        in_specs=[SMEM, VMEM],
        out_specs=VMEM,
        compiler_params=PARAMS,
        name="pick_screened",
    )(cell_map, screened)


def cut_kernel(s, me_ref, green_ref, *greens):
    me = me_ref[0]
    for k in range(s.groups):
        cell, part, lanes = s.where(me ^ k)
        for comp in range(s.comps):
            for j in range(s.energies):
                if s.parts == 1:
                    greens[k][comp * s.energies + j] = green_ref[comp, j, cell, :, lanes]
                else:
                    value = green_ref[comp, j, cell, :, lanes].astype(jnp.float32)
                    greens[k][comp * s.energies + j] = part_of(s, value, part).astype(greens[k].dtype)


def cut_green(s, me, green):
    return pl.pallas_call(
        functools.partial(cut_kernel, s),
        out_shape=[jax.ShapeDtypeStruct((s.planes,) + s.plane, green.dtype)] * s.groups,
        in_specs=[SMEM, VMEM],
        out_specs=[VMEM] * s.groups,
        compiler_params=PARAMS,
        name="cut_green",
    )(me, green)


def held(s):
    return jax.ShapeDtypeStruct((s.comps, (s.groups // 2 + 2) * s.energies) + s.plane, jnp.float32)


def stage_green(s, me, first, blocks, g_half):
    half = s.groups // 2
    zero = jnp.zeros(s.plane, jnp.float32)
    for comp in range(s.comps):
        for j in range(s.energies):
            g_half[comp, j] = zero
            g_half[comp, (half + 1) * s.energies + j] = zero
            for k, block in enumerate(blocks):
                group = (me ^ (first + k)) % half
                g_half[comp, (group + 1) * s.energies + j] = block[comp * s.energies + j].astype(jnp.float32)


def stage_near_kernel(s, me_ref, screens_ref, *refs):
    g_half, w_all = refs[-2:]
    stage_green(s, me_ref[0], 0, refs[:-2], g_half)
    for comp in range(s.comps):
        for j in range(s.energies):
            plane = comp * s.energies + j
            for source in range(s.groups):
                if s.parts > 1:
                    w_all[source, comp, j] = screens_ref[source, plane].astype(jnp.float32)
                    continue
                for c in range(s.cells):
                    piece = screens_ref[source * s.cells + c, plane].astype(jnp.float32)
                    w_all[source, comp, j, c * s.held : (c + 1) * s.held, :] = piece


def stage_near(s, me, screens, greens):
    return pl.pallas_call(
        functools.partial(stage_near_kernel, s),
        out_shape=[held(s), jax.ShapeDtypeStruct((s.groups, s.comps, s.energies) + s.plane, jnp.float32)],
        in_specs=[SMEM] + [VMEM] * (len(greens) + 1),
        out_specs=[VMEM] * 2,
        compiler_params=PARAMS,
        name="stage_near",
    )(me, screens, *greens)


def stage_far_kernel(s, me_ref, after_ref, *refs):
    stage_green(s, me_ref[0], s.groups // 2, refs[:-1], refs[-1])


def stage_far(s, me, greens, after):
    return pl.pallas_call(
        functools.partial(stage_far_kernel, s),
        out_shape=held(s),
        in_specs=[SMEM, ANY] + [VMEM] * len(greens),
        out_specs=VMEM,
        compiler_params=PARAMS,
        name="stage_far",
    )(me, after, *greens)


def add_terms(s, slots, side, group, kind, table_ref, count_ref, g_half, w_all, sums):
    low = side * (s.groups // 2)

    def turn(source, sums):
        sums = list(sums)
        count = count_ref[group, source]
        for slot in range(slots):
            shift = jnp.clip(table_ref[group * s.groups + source, slot], 0, s.energies - 1)
            live = jnp.where(slot < count, 1.0, 0.0).astype(jnp.float32)
            start = (group - source - low + 1) * s.energies - shift
            w_real = w_all[source, 2 * kind, shift] * live
            w_imag = w_all[source, 2 * kind + 1, shift] * live
            for j in range(s.energies):
                g_real = g_half[2 * kind, start + j]
                g_imag = g_half[2 * kind + 1, start + j]
                sums[j] = sums[j] - (g_real * w_imag + g_imag * w_real)
                sums[s.energies + j] = sums[s.energies + j] + (g_real * w_real - g_imag * w_imag)
        return tuple(sums)

    first = jnp.maximum(group - low - s.groups // 2, 0)
    return lax.fori_loop(first, jnp.maximum(group - low + 1, first), turn, tuple(sums))


def partial_kernel(s, slots, ks, me_ref, table_ref, count_ref, g_half, w_all, out_ref):
    me = me_ref[0]
    side = me // (s.groups // 2)
    for at, k in enumerate(ks):
        for kind in range(2):
            zeros = [jnp.zeros(s.plane, jnp.float32) for _ in range(2 * s.energies)]
            sums = add_terms(s, slots, side, me ^ k, kind, table_ref, count_ref, g_half, w_all, zeros)
            for j, total in enumerate(sums):
                out_ref[at, kind * 2 * s.energies + j] = total


def partial_of(s, me, table, count, g_half, w_all, ks):
    return pl.pallas_call(
        functools.partial(partial_kernel, s, table.shape[1], ks),
        out_shape=jax.ShapeDtypeStruct((len(ks), s.planes) + s.plane, jnp.float32),
        in_specs=[SMEM] * 3 + [VMEM] * 2,
        out_specs=VMEM,
        compiler_params=PARAMS,
        name="partial",
    )(me, table, count, g_half, w_all)


def sigma_kernel(s, slots, ks, begun, me_ref, table_ref, count_ref, *refs):
    outs = refs[-len(ks) :]
    other, w_all, g_far = refs[: -len(ks)]
    me = me_ref[0]
    side = me // (s.groups // 2)
    row = lax.broadcasted_iota(jnp.int32, s.plane, 0)
    for at, k in enumerate(ks):
        group = me ^ k
        codes = [jnp.zeros(s.plane, jnp.float32) for _ in range(s.scale_planes)]
        for kind in range(2):
            first = kind * 2 * s.energies
            if begun is None:
                sums = [jnp.zeros(s.plane, jnp.float32) for _ in range(2 * s.energies)]
                sums = add_terms(s, slots, side, group, kind, table_ref, count_ref, other, w_all, sums)
            else:
                sums = [other[begun + at, first + j] for j in range(2 * s.energies)]
            sums = add_terms(s, slots, 1 - side, group, kind, table_ref, count_ref, g_far, w_all, sums)
            sums = [total * SCALE for total in sums]
            if k == 0:
                for j, total in enumerate(sums):
                    outs[at][first + j] = total
                continue
            for low in range(0, 2 * s.energies, PAIR):
                pair = sums[low : low + PAIR]
                largest = functools.reduce(jnp.maximum, [jnp.abs(total) for total in pair])
                largest = jnp.maximum(jnp.max(largest, axis=0, keepdims=True), TINY)
                code = jnp.ceil(jnp.log2(largest) * FINE)
                inverse = jnp.exp2(code * (-1.0 / FINE)) * halfS
                where = (first + low) // PAIR
                spot = where // s.plane[0]
                codes[spot] = jnp.where(row == where % s.plane[0], code, codes[spot])
                for j, total in enumerate(pair):
                    coded = jnp.round(total * inverse).astype(jnp.int32)
                    outs[at][first + low + j] = coded.astype(jnp.int16)
        if k != 0:
            for j in range(s.scale_planes):
                outs[at][s.planes + j] = codes[j].astype(jnp.int32).astype(jnp.int16)


def sigma_of(s, me, table, count, g_far, w_all, other, ks, begun):
    own = jax.ShapeDtypeStruct((s.planes,) + s.plane, jnp.float32)
    coded = jax.ShapeDtypeStruct((s.planes + s.scale_planes,) + s.plane, jnp.int16)
    return pl.pallas_call(
        functools.partial(sigma_kernel, s, table.shape[1], ks, begun),
        out_shape=[own if k == 0 else coded for k in ks],
        in_specs=[SMEM] * 3 + [VMEM] * 3,
        out_specs=[VMEM] * len(ks),
        compiler_params=PARAMS,
        name="sigma",
    )(me, table, count, other, w_all, g_far)


def unpack_kernel(s, me_ref, *refs):
    blocks, whole_ref = refs[: s.groups], refs[s.groups]
    me = me_ref[0]
    for k, block in enumerate(blocks):
        cell, part, lanes = s.where(me ^ k)
        rows = slice(None) if s.parts == 1 else pl.ds(pl.multiple_of(part * s.plane[0], s.plane[0]), s.plane[0])
        scales = []
        if k != 0:
            for j in range(s.scale_planes):
                code = block[s.planes + j].astype(jnp.int32).astype(jnp.float32)
                scales.append(jnp.exp2(code * (1.0 / FINE)) * (1.0 / halfS))
        for comp in range(s.comps):
            for j in range(s.energies):
                plane = comp * s.energies + j
                value = block[plane]
                if k != 0:
                    where = plane // PAIR
                    scale = scales[where // s.plane[0]][where % s.plane[0] : where % s.plane[0] + 1]
                    value = value.astype(jnp.int32).astype(jnp.float32) * scale
                whole_ref[comp, j, cell, rows, lanes] = value


def unpack(s, me, blocks):
    return pl.pallas_call(
        functools.partial(unpack_kernel, s),
        out_shape=jax.ShapeDtypeStruct((s.comps, s.energies, s.per_cell, s.rows, s.width), jnp.float32),
        in_specs=[SMEM] + [VMEM] * s.groups,
        out_specs=VMEM,
        compiler_params=PARAMS,
        name="unpack",
    )(me, *blocks)


def swap(s, block, k):
    return block if k == 0 else lax.ppermute(block, "energy", [(i, i ^ k) for i in range(s.groups)])


def send_screened(s, cell_map, screened):
    if s.parts == 1:
        return lax.all_to_all(pick_screened(s, cell_map, screened), ("energy", "cell"), 0, 0, tiled=True)
    chosen = jnp.take(screened, cell_map, axis=2).reshape(s.planes, s.cells, s.per_cell, s.held, s.width)
    whole = lax.all_to_all(chosen, "cell", 1, 3, tiled=True)
    cut = whole.reshape(s.planes, s.per_cell, s.parts, s.plane[0], s.tiles, LANES)
    cut = jnp.transpose(cut, (1, 4, 2, 0, 3, 5)).reshape((s.groups, s.planes) + s.plane)
    return lax.all_to_all(cut, "energy", 0, 0, tiled=True)


def per_device(green, screened, cell_map, shift_table, shift_count):
    s = Sizes(green, screened, lax.axis_size("energy"), lax.axis_size("cell"))
    me = jnp.stack([lax.axis_index("energy"), lax.axis_index("cell")]).astype(jnp.int32)
    half = s.groups // 2
    far, near = list(range(half, s.groups)), list(range(half))

    screens = send_screened(s, cell_map, screened)
    greens = [swap(s, block, k) for k, block in enumerate(cut_green(s, me, green))]
    table = shift_table.reshape(s.groups * s.groups, shift_table.shape[2])
    g_near, w_all = stage_near(s, me, screens, greens[:half])
    begun = partial_of(s, me, table, shift_count, g_near, w_all, far)
    g_far = stage_far(s, me, greens[half:], begun)
    sums = {}
    for first in range(0, half, half):
        ks = far[first : first + half]
        for k, block in zip(ks, sigma_of(s, me, table, shift_count, g_far, w_all, begun, ks, first)):
            sums[k] = swap(s, block, k)
    for k, block in zip(near, sigma_of(s, me, table, shift_count, g_far, w_all, g_near, near, None)):
        sums[k] = swap(s, block, k)
    return unpack(s, me, [sums[k] for k in range(s.groups)])


def solution(mesh):
    placed = (
        P(None, "energy", "cell", None, None),
        P(None, "energy", None, "cell", None),
        P(),
        P(),
        P(),
    )
    return jax.shard_map(
        per_device,
        mesh=mesh,
        in_specs=placed,
        out_specs=P(None, "energy", "cell", None, None),
        check_vma=False,
    )
```

```python
import functools

import jax
import jax.numpy as jnp
from jax import lax
from jax.experimental import pallas as pl
from jax.experimental.pallas import tpu as pltpu
from jax.sharding import PartitionSpec as P

SCALE = 0.2
LANES = 128
PAIR = 2
STEPS = 32700.0
FINE = 64.0
TINY = 1e-34
SMEM = pl.BlockSpec(memory_space=pltpu.SMEM)
VMEM = pl.BlockSpec(memory_space=pltpu.VMEM)
ANY = pl.BlockSpec(memory_space=pl.ANY)
PARAMS = pltpu.CompilerParams(vmem_limit_bytes=32 * 1024 * 1024)


class Sizes:
    def __init__(self, green, screened, groups, cells):
        self.comps, self.energies, self.per_cell, self.rows, self.width = green.shape
        self.groups, self.cells = groups, cells
        self.tiles = self.width // LANES
        self.slices = groups // self.per_cell
        self.parts = self.slices // self.tiles
        self.held = screened.shape[3]
        self.plane = (self.rows // self.parts, LANES)
        self.planes = self.comps * self.energies
        self.half = groups // 2
        self.held_planes = (self.half + 2) * self.energies
        self.scales = self.planes // PAIR
        self.scale_planes = -(-self.scales // self.plane[0])

    def where(self, index):
        cell, tile, part = index // self.slices, (index // self.parts) % self.tiles, index % self.parts
        return cell, part, pl.ds(pl.multiple_of(tile * LANES, LANES), LANES)


def part_of(s, value, part):
    count = value.shape[0] // s.parts
    chosen = value[:count]
    for other in range(1, s.parts):
        chosen = jnp.where(part == other, value[other * count : (other + 1) * count], chosen)
    return chosen


def pick_kernel(s, map_hbm, screened_hbm, out_hbm, map_ref, screened_ref, out_ref, in_sems, out_sems, map_sem):
    chunks = [pl.ds(comp * s.energies, s.energies) for comp in range(s.comps)]
    arriving = [
        pltpu.make_async_copy(screened_hbm.at[chunk], screened_ref.at[chunk], in_sems.at[i])
        for i, chunk in enumerate(chunks)
    ]
    leaving = [
        pltpu.make_async_copy(out_ref.at[:, chunk], out_hbm.at[:, chunk], out_sems.at[i])
        for i, chunk in enumerate(chunks)
    ]
    mapped = pltpu.make_async_copy(map_hbm, map_ref, map_sem)
    mapped.start()
    for copy in arriving:
        copy.start()
    mapped.wait()
    picked = [map_ref[i] for i in range(s.cells * s.per_cell)]
    for comp in range(s.comps):
        arriving[comp].wait()
        for plane in range(comp * s.energies, (comp + 1) * s.energies):
            for i, cell in enumerate(picked):
                for t in range(s.tiles):
                    target = (i % s.per_cell * s.slices + t) * s.cells + i // s.per_cell
                    out_ref[target, plane] = screened_ref[plane, cell, :, t * LANES : (t + 1) * LANES]
        leaving[comp].start()
    for copy in leaving:
        copy.wait()


def pick_screened(s, cell_map, screened):
    out = jax.ShapeDtypeStruct((s.groups * s.cells, s.planes, s.held, LANES), screened.dtype)
    flat = screened.reshape((s.planes,) + screened.shape[2:])
    return pl.pallas_call(
        functools.partial(pick_kernel, s),
        out_shape=out,
        in_specs=[ANY, ANY],
        out_specs=ANY,
        scratch_shapes=[
            pltpu.SMEM(cell_map.shape, jnp.int32),
            pltpu.VMEM(flat.shape, flat.dtype),
            pltpu.VMEM(out.shape, out.dtype),
            pltpu.SemaphoreType.DMA((s.comps,)),
            pltpu.SemaphoreType.DMA((s.comps,)),
            pltpu.SemaphoreType.DMA(()),
        ],
        compiler_params=pltpu.CompilerParams(vmem_limit_bytes=60 * 1024 * 1024),
        name="pick_screened",
    )(cell_map, flat)


def cut_kernel(s, me_ref, green_ref, *greens):
    me = me_ref[0]
    places = [s.where(me ^ k) for k in range(s.groups)]

    for plane in range(s.planes):
        for k, (cell, part, lanes) in enumerate(places):
            value = green_ref[plane, cell, :, lanes]
            if s.parts > 1:
                value = part_of(s, value.astype(jnp.float32), part).astype(greens[k].dtype)
            greens[k][plane] = value


def cut_green(s, me, green):
    return pl.pallas_call(
        functools.partial(cut_kernel, s),
        out_shape=[jax.ShapeDtypeStruct((s.planes,) + s.plane, green.dtype)] * s.groups,
        in_specs=[SMEM, VMEM],
        out_specs=[VMEM] * s.groups,
        compiler_params=PARAMS,
        name="cut_green",
    )(me, green.reshape((s.planes,) + green.shape[2:]))


def held(s):
    return jax.ShapeDtypeStruct((s.comps * s.held_planes,) + s.plane, jnp.float32)


def stage_green(s, me, first, blocks, g_half):
    zero = jnp.zeros(s.plane, jnp.float32)
    spots = [((me ^ (first + k)) % s.half + 1) * s.energies for k in range(s.half)]

    @pl.loop(0, s.energies)
    def _(j):
        for comp in range(s.comps):
            base = comp * s.held_planes + j
            g_half[base] = zero
            g_half[base + (s.half + 1) * s.energies] = zero
            for spot, block in zip(spots, blocks):
                g_half[base + spot] = block[comp * s.energies + j].astype(jnp.float32)


def stage_near_kernel(s, me_ref, screens_ref, *refs):
    g_half, w_all = refs[-2:]
    stage_green(s, me_ref[0], 0, refs[:-2], g_half)

    @pl.loop(0, s.planes)
    def _(plane):
        for source in range(s.groups):
            if s.parts > 1:
                w_all[source, plane] = screens_ref[source, plane].astype(jnp.float32)
                continue
            for c in range(s.cells):
                piece = screens_ref[source * s.cells + c, plane].astype(jnp.float32)
                w_all[source, plane, c * s.held : (c + 1) * s.held, :] = piece


def stage_near(s, me, screens, greens):
    return pl.pallas_call(
        functools.partial(stage_near_kernel, s),
        out_shape=[held(s), jax.ShapeDtypeStruct((s.groups, s.planes) + s.plane, jnp.float32)],
        in_specs=[SMEM] + [VMEM] * (len(greens) + 1),
        out_specs=[VMEM] * 2,
        compiler_params=PARAMS,
        name="stage_near",
    )(me, screens, *greens)


def stage_far_kernel(s, me_ref, after_ref, *refs):
    stage_green(s, me_ref[0], s.groups // 2, refs[:-1], refs[-1])


def stage_far(s, me, greens, after):
    return pl.pallas_call(
        functools.partial(stage_far_kernel, s),
        out_shape=held(s),
        in_specs=[SMEM, ANY] + [VMEM] * len(greens),
        out_specs=VMEM,
        compiler_params=PARAMS,
        name="stage_far",
    )(me, after, *greens)


def add_terms(s, slots, side, group, kind, table_ref, count_ref, g_half, w_all, sums):
    low = side * s.half
    real, imag = 2 * kind, 2 * kind + 1

    def turn(source, sums):
        sums = list(sums)
        count = count_ref[group, source]
        for slot in range(slots):
            shift = jnp.clip(table_ref[group * s.groups + source, slot], 0, s.energies - 1)
            live = jnp.where(slot < count, 1.0, 0.0).astype(jnp.float32)
            start = (group - source - low + 1) * s.energies - shift
            w_real = w_all[source, real * s.energies + shift] * live
            w_imag = w_all[source, imag * s.energies + shift] * live
            for j in range(s.energies):
                g_real = g_half[real * s.held_planes + start + j]
                g_imag = g_half[imag * s.held_planes + start + j]
                sums[j] = sums[j] - (g_real * w_imag + g_imag * w_real)
                sums[s.energies + j] = sums[s.energies + j] + (g_real * w_real - g_imag * w_imag)
        return tuple(sums)

    first = jnp.maximum(group - low - s.half, 0)
    return lax.fori_loop(first, jnp.maximum(group - low + 1, first), turn, tuple(sums))


def partial_kernel(s, slots, me_ref, table_ref, count_ref, g_half, w_all, out_ref):
    me = me_ref[0]

    @pl.loop(0, 2 * s.groups)
    def _(at):
        k, kind = at // 2, at % 2
        zeros = [jnp.zeros(s.plane, jnp.float32) for _ in range(2 * s.energies)]
        sums = add_terms(s, slots, me // s.half, me ^ k, kind, table_ref, count_ref, g_half, w_all, zeros)
        for j, total in enumerate(sums):
            out_ref[k, kind * 2 * s.energies + j] = total


def partial_of(s, me, table, count, g_half, w_all):
    return pl.pallas_call(
        functools.partial(partial_kernel, s, table.shape[1]),
        out_shape=jax.ShapeDtypeStruct((s.groups, s.planes) + s.plane, jnp.float32),
        in_specs=[SMEM] * 3 + [VMEM] * 2,
        out_specs=VMEM,
        compiler_params=PARAMS,
        name="partial",
    )(me, table, count, g_half, w_all)


def sigma_kernel(s, slots, ks, me_ref, table_ref, count_ref, begun, w_all, g_far, *outs):
    me = me_ref[0]
    side = me // s.half
    row = lax.broadcasted_iota(jnp.int32, s.plane, 0)
    for at, k in enumerate(ks):

        def turn(kind, codes):
            codes = list(codes)
            first = kind * 2 * s.energies
            sums = [begun[k, first + j] for j in range(2 * s.energies)]
            sums = add_terms(s, slots, 1 - side, me ^ k, kind, table_ref, count_ref, g_far, w_all, sums)
            sums = [total * SCALE for total in sums]
            if k == 0:
                for j, total in enumerate(sums):
                    outs[at][first + j] = total
                return tuple(codes)
            for low in range(0, 2 * s.energies, PAIR):
                pair = sums[low : low + PAIR]
                largest = functools.reduce(jnp.maximum, [jnp.abs(total) for total in pair])
                largest = jnp.maximum(jnp.max(largest, axis=0, keepdims=True), TINY)
                code = jnp.ceil(jnp.log2(largest) * FINE)
                inverse = jnp.exp2(code * (-1.0 / FINE)) * STEPS
                where = (first + low) // PAIR
                for i in range(s.scale_planes):
                    codes[i] = jnp.where(row + i * s.plane[0] == where, code, codes[i])
                for j, total in enumerate(pair):
                    coded = jnp.round(total * inverse).astype(jnp.int32)
                    outs[at][first + low + j] = coded.astype(jnp.int16)
            return tuple(codes)

        codes = lax.fori_loop(0, 2, turn, tuple(jnp.zeros(s.plane, jnp.float32) for _ in range(s.scale_planes)))
        if k != 0:
            for j in range(s.scale_planes):
                outs[at][s.planes + j] = codes[j].astype(jnp.int32).astype(jnp.int16)


def sigma_of(s, me, table, count, begun, w_all, g_far, ks):
    own = jax.ShapeDtypeStruct((s.planes,) + s.plane, jnp.float32)
    coded = jax.ShapeDtypeStruct((s.planes + s.scale_planes,) + s.plane, jnp.int16)
    return pl.pallas_call(
        functools.partial(sigma_kernel, s, table.shape[1], ks),
        out_shape=[own if k == 0 else coded for k in ks],
        in_specs=[SMEM] * 3 + [VMEM] * 3,
        out_specs=[VMEM] * len(ks),
        compiler_params=PARAMS,
        name="sigma",
    )(me, table, count, begun, w_all, g_far)


def unpack_kernel(s, order, me_ref, *refs):
    at = dict(zip(order, refs))
    blocks, whole_ref, scales = [at[k] for k in range(s.groups)], refs[s.groups], refs[s.groups + 1]
    me = me_ref[0]
    places = []
    for k, block in enumerate(blocks):
        cell, part, lanes = s.where(me ^ k)
        places.append((cell, slice(None) if s.parts == 1 else pl.ds(pl.multiple_of(part * s.plane[0], s.plane[0]), s.plane[0]), lanes))
        if k != 0:
            for j in range(s.scale_planes):
                code = block[s.planes + j].astype(jnp.int32).astype(jnp.float32)
                scales[k, j * s.plane[0] : (j + 1) * s.plane[0]] = jnp.exp2(code * (1.0 / FINE)) * (1.0 / STEPS)

    @pl.loop(0, s.scales)
    def _(pair):
        for k, (cell, rows, lanes) in enumerate(places):
            for i in range(PAIR):
                value = blocks[k][pair * PAIR + i]
                if k != 0:
                    value = value.astype(jnp.int32).astype(jnp.float32) * scales[k, pl.ds(pair, 1)]
                whole_ref[pair * PAIR + i, cell, rows, lanes] = value


def unpack(s, me, blocks, order):
    return pl.pallas_call(
        functools.partial(unpack_kernel, s, order),
        out_shape=jax.ShapeDtypeStruct((s.planes, s.per_cell, s.rows, s.width), jnp.float32),
        in_specs=[SMEM] + [VMEM] * s.groups,
        out_specs=VMEM,
        scratch_shapes=[pltpu.VMEM((s.groups, s.scale_planes * s.plane[0], LANES), jnp.float32)],
        compiler_params=PARAMS,
        name="unpack",
    )(me, *[blocks[k] for k in order])


def swap(s, block, k):
    return block if k == 0 else lax.ppermute(block, "energy", [(i, i ^ k) for i in range(s.groups)])


def send_screened(s, cell_map, screened):
    if s.parts == 1:
        return lax.all_to_all(pick_screened(s, cell_map, screened), ("energy", "cell"), 0, 0, tiled=True)
    chosen = jnp.take(screened, cell_map, axis=2).reshape(s.planes, s.cells, s.per_cell, s.held, s.width)
    whole = lax.all_to_all(chosen, "cell", 1, 3, tiled=True)
    cut = whole.reshape(s.planes, s.per_cell, s.parts, s.plane[0], s.tiles, LANES)
    cut = jnp.transpose(cut, (1, 4, 2, 0, 3, 5)).reshape((s.groups, s.planes) + s.plane)
    return lax.all_to_all(cut, "energy", 0, 0, tiled=True)


def per_device(green, screened, cell_map, shift_table, shift_count):
    s = Sizes(green, screened, lax.axis_size("energy"), lax.axis_size("cell"))
    me = lax.axis_index("energy").astype(jnp.int32).reshape(1)
    half = s.groups // 2
    far, near = list(range(half, s.groups)), list(range(half))

    screens = send_screened(s, cell_map, screened)
    greens = [swap(s, block, k) for k, block in enumerate(cut_green(s, me, green))]
    table = shift_table.reshape(s.groups * s.groups, shift_table.shape[2])
    g_near, w_all = stage_near(s, me, screens, greens[:half])
    begun = partial_of(s, me, table, shift_count, g_near, w_all)
    g_far = stage_far(s, me, greens[half:], begun)
    first, later = far[:2], [0] + far[2:] + near[1:]
    sums = {}
    for ks in (first, later):
        for k, block in zip(ks, sigma_of(s, me, table, shift_count, begun, w_all, g_far, ks)):
            sums[k] = swap(s, block, k)
    return unpack(s, me, sums, later + first).reshape(green.shape)


def solution(mesh):
    placed = (
        P(None, "energy", "cell", None, None),
        P(None, "energy", None, "cell", None),
        P(),
        P(),
        P(),
    )
    return jax.shard_map(
        per_device,
        mesh=mesh,
        in_specs=placed,
        out_specs=P(None, "energy", "cell", None, None),
        check_vma=False,
    )
```

```python
import functools

import jax
import jax.numpy as jnp
from jax import lax
from jax.experimental import pallas as pl
from jax.experimental.pallas import tpu as pltpu
from jax.sharding import PartitionSpec as P

SCALE = 0.2
LANES = 128
PAIR = 2
STEPS = 32700.0
FINE = 64.0
TINY = 1e-34
PICKS = 8
SMEM = pl.BlockSpec(memory_space=pltpu.SMEM)
VMEM = pl.BlockSpec(memory_space=pltpu.VMEM)
ANY = pl.BlockSpec(memory_space=pl.ANY)
PARAMS = pltpu.CompilerParams(vmem_limit_bytes=32 * 1024 * 1024)


class Sizes:
    def __init__(self, green, screened, groups, cells):
        self.comps, self.energies, self.per_cell, self.rows, self.width = green.shape
        self.groups, self.cells = groups, cells
        self.tiles = self.width // LANES
        self.slices = groups // self.per_cell
        self.parts = self.slices // self.tiles
        self.held = screened.shape[3]
        self.plane = (self.rows // self.parts, LANES)
        self.planes = self.comps * self.energies
        self.half = groups // 2
        self.held_planes = (self.half + 2) * self.energies
        self.scales = self.planes // PAIR
        self.scale_planes = -(-self.scales // self.plane[0])

    def where(self, index):
        cell, tile, part = index // self.slices, (index // self.parts) % self.tiles, index % self.parts
        return cell, part, pl.ds(pl.multiple_of(tile * LANES, LANES), LANES)


def part_of(s, value, part):
    count = value.shape[0] // s.parts
    chosen = value[:count]
    for other in range(1, s.parts):
        chosen = jnp.where(part == other, value[other * count : (other + 1) * count], chosen)
    return chosen


def pick_kernel(s, map_hbm, screened_hbm, out_hbm, map_ref, screened_ref, out_ref, in_sems, out_sems, map_sem):
    size = s.planes // PICKS
    chunks = [pl.ds(i * size, size) for i in range(PICKS)]
    arriving = [
        pltpu.make_async_copy(screened_hbm.at[chunk], screened_ref.at[chunk], in_sems.at[i])
        for i, chunk in enumerate(chunks)
    ]
    leaving = [
        pltpu.make_async_copy(out_ref.at[:, chunk], out_hbm.at[:, chunk], out_sems.at[i])
        for i, chunk in enumerate(chunks)
    ]
    mapped = pltpu.make_async_copy(map_hbm, map_ref, map_sem)
    mapped.start()
    for copy in arriving:
        copy.start()
    mapped.wait()
    picked = [map_ref[i] for i in range(s.cells * s.per_cell)]
    for chunk in range(PICKS):
        arriving[chunk].wait()
        for plane in range(chunk * size, (chunk + 1) * size):
            for i, cell in enumerate(picked):
                for t in range(s.tiles):
                    target = (i % s.per_cell * s.slices + t) * s.cells + i // s.per_cell
                    out_ref[target, plane] = screened_ref[plane, cell, :, t * LANES : (t + 1) * LANES]
        leaving[chunk].start()
    for copy in leaving:
        copy.wait()


def pick_screened(s, cell_map, screened):
    out = jax.ShapeDtypeStruct((s.groups * s.cells, s.planes, s.held, LANES), screened.dtype)
    flat = screened.reshape((s.planes,) + screened.shape[2:])
    return pl.pallas_call(
        functools.partial(pick_kernel, s),
        out_shape=out,
        in_specs=[ANY, ANY],
        out_specs=ANY,
        scratch_shapes=[
            pltpu.SMEM(cell_map.shape, jnp.int32),
            pltpu.VMEM(flat.shape, flat.dtype),
            pltpu.VMEM(out.shape, out.dtype),
            pltpu.SemaphoreType.DMA((PICKS,)),
            pltpu.SemaphoreType.DMA((PICKS,)),
            pltpu.SemaphoreType.DMA(()),
        ],
        compiler_params=pltpu.CompilerParams(vmem_limit_bytes=60 * 1024 * 1024),
        name="pick_screened",
    )(cell_map, flat)


def cut_kernel(s, me_ref, green_ref, *greens):
    me = me_ref[0]
    places = [s.where(me ^ k) for k in range(s.groups)]

    for plane in range(s.planes):
        for k, (cell, part, lanes) in enumerate(places):
            value = green_ref[plane, cell, :, lanes]
            if s.parts > 1:
                value = part_of(s, value.astype(jnp.float32), part).astype(greens[k].dtype)
            greens[k][plane] = value


def cut_green(s, me, green):
    return pl.pallas_call(
        functools.partial(cut_kernel, s),
        out_shape=[jax.ShapeDtypeStruct((s.planes,) + s.plane, green.dtype)] * s.groups,
        in_specs=[SMEM, VMEM],
        out_specs=[VMEM] * s.groups,
        compiler_params=PARAMS,
        name="cut_green",
    )(me, green.reshape((s.planes,) + green.shape[2:]))


def held(s):
    return jax.ShapeDtypeStruct((s.comps * s.held_planes,) + s.plane, jnp.float32)


def stage_green(s, me, first, blocks, g_half):
    zero = jnp.zeros(s.plane, jnp.float32)
    spots = [((me ^ (first + k)) % s.half + 1) * s.energies for k in range(s.half)]

    @pl.loop(0, s.energies)
    def _(j):
        for comp in range(s.comps):
            base = comp * s.held_planes + j
            g_half[base] = zero
            g_half[base + (s.half + 1) * s.energies] = zero
            for spot, block in zip(spots, blocks):
                g_half[base + spot] = block[comp * s.energies + j].astype(jnp.float32)


def stage_near_kernel(s, me_ref, screens_ref, *refs):
    g_half, w_all = refs[-2:]
    stage_green(s, me_ref[0], 0, refs[:-2], g_half)

    @pl.loop(0, s.planes)
    def _(plane):
        for source in range(s.groups):
            if s.parts > 1:
                w_all[source, plane] = screens_ref[source, plane].astype(jnp.float32)
                continue
            for c in range(s.cells):
                piece = screens_ref[source * s.cells + c, plane].astype(jnp.float32)
                w_all[source, plane, c * s.held : (c + 1) * s.held, :] = piece


def stage_near(s, me, screens, greens):
    return pl.pallas_call(
        functools.partial(stage_near_kernel, s),
        out_shape=[held(s), jax.ShapeDtypeStruct((s.groups, s.planes) + s.plane, jnp.float32)],
        in_specs=[SMEM] + [VMEM] * (len(greens) + 1),
        out_specs=[VMEM] * 2,
        compiler_params=PARAMS,
        name="stage_near",
    )(me, screens, *greens)


def stage_far_kernel(s, me_ref, after_ref, *refs):
    stage_green(s, me_ref[0], s.groups // 2, refs[:-1], refs[-1])


def stage_far(s, me, greens, after):
    return pl.pallas_call(
        functools.partial(stage_far_kernel, s),
        out_shape=held(s),
        in_specs=[SMEM, ANY] + [VMEM] * len(greens),
        out_specs=VMEM,
        compiler_params=PARAMS,
        name="stage_far",
    )(me, after, *greens)


def add_terms(s, slots, side, group, kind, table_ref, count_ref, g_half, w_all, sums):
    low = side * s.half
    real, imag = 2 * kind, 2 * kind + 1

    def turn(source, sums):
        sums = list(sums)
        count = count_ref[group, source]
        for slot in range(slots):
            shift = jnp.clip(table_ref[group * s.groups + source, slot], 0, s.energies - 1)
            live = jnp.where(slot < count, 1.0, 0.0).astype(jnp.float32)
            start = (group - source - low + 1) * s.energies - shift
            w_real = w_all[source, real * s.energies + shift] * live
            w_imag = w_all[source, imag * s.energies + shift] * live
            for j in range(s.energies):
                g_real = g_half[real * s.held_planes + start + j]
                g_imag = g_half[imag * s.held_planes + start + j]
                sums[j] = sums[j] - (g_real * w_imag + g_imag * w_real)
                sums[s.energies + j] = sums[s.energies + j] + (g_real * w_real - g_imag * w_imag)
        return tuple(sums)

    first = jnp.maximum(group - low - s.half, 0)
    return lax.fori_loop(first, jnp.maximum(group - low + 1, first), turn, tuple(sums))


def partial_kernel(s, slots, me_ref, table_ref, count_ref, g_half, w_all, out_ref):
    me = me_ref[0]

    @pl.loop(0, 2 * s.groups)
    def _(at):
        k, kind = at // 2, at % 2
        zeros = [jnp.zeros(s.plane, jnp.float32) for _ in range(2 * s.energies)]
        sums = add_terms(s, slots, me // s.half, me ^ k, kind, table_ref, count_ref, g_half, w_all, zeros)
        for j, total in enumerate(sums):
            out_ref[k, kind * 2 * s.energies + j] = total


def partial_of(s, me, table, count, g_half, w_all):
    return pl.pallas_call(
        functools.partial(partial_kernel, s, table.shape[1]),
        out_shape=jax.ShapeDtypeStruct((s.groups, s.planes) + s.plane, jnp.float32),
        in_specs=[SMEM] * 3 + [VMEM] * 2,
        out_specs=VMEM,
        compiler_params=PARAMS,
        name="partial",
    )(me, table, count, g_half, w_all)


def sigma_kernel(s, slots, ks, me_ref, table_ref, count_ref, begun, w_all, g_far, *outs):
    me = me_ref[0]
    side = me // s.half
    row = lax.broadcasted_iota(jnp.int32, s.plane, 0)
    for at, k in enumerate(ks):

        def turn(kind, codes):
            codes = list(codes)
            first = kind * 2 * s.energies
            sums = [begun[k, first + j] for j in range(2 * s.energies)]
            sums = add_terms(s, slots, 1 - side, me ^ k, kind, table_ref, count_ref, g_far, w_all, sums)
            sums = [total * SCALE for total in sums]
            if k == 0:
                for j, total in enumerate(sums):
                    outs[at][first + j] = total
                return tuple(codes)
            for low in range(0, 2 * s.energies, PAIR):
                pair = sums[low : low + PAIR]
                largest = functools.reduce(jnp.maximum, [jnp.abs(total) for total in pair])
                largest = jnp.maximum(jnp.max(largest, axis=0, keepdims=True), TINY)
                code = jnp.ceil(jnp.log2(largest) * FINE)
                inverse = jnp.exp2(code * (-1.0 / FINE)) * STEPS
                where = (first + low) // PAIR
                for i in range(s.scale_planes):
                    codes[i] = jnp.where(row + i * s.plane[0] == where, code, codes[i])
                for j, total in enumerate(pair):
                    coded = jnp.round(total * inverse).astype(jnp.int32)
                    outs[at][first + low + j] = coded.astype(jnp.int16)
            return tuple(codes)

        codes = lax.fori_loop(0, 2, turn, tuple(jnp.zeros(s.plane, jnp.float32) for _ in range(s.scale_planes)))
        if k != 0:
            for j in range(s.scale_planes):
                outs[at][s.planes + j] = codes[j].astype(jnp.int32).astype(jnp.int16)


def sigma_of(s, me, table, count, begun, w_all, g_far, ks):
    own = jax.ShapeDtypeStruct((s.planes,) + s.plane, jnp.float32)
    coded = jax.ShapeDtypeStruct((s.planes + s.scale_planes,) + s.plane, jnp.int16)
    return pl.pallas_call(
        functools.partial(sigma_kernel, s, table.shape[1], ks),
        out_shape=[own if k == 0 else coded for k in ks],
        in_specs=[SMEM] * 3 + [VMEM] * 3,
        out_specs=[VMEM] * len(ks),
        compiler_params=PARAMS,
        name="sigma",
    )(me, table, count, begun, w_all, g_far)


def unpack_kernel(s, order, me_ref, *refs):
    at = dict(zip(order, refs))
    blocks = [at[k] for k in range(s.groups)]
    whole_hbm, whole_ref, scales, sems = refs[s.groups :]
    me = me_ref[0]
    places = []
    for k, block in enumerate(blocks):
        cell, part, lanes = s.where(me ^ k)
        rows = slice(None) if s.parts == 1 else pl.ds(pl.multiple_of(part * s.plane[0], s.plane[0]), s.plane[0])
        places.append((cell, rows, lanes))
        if k != 0:
            for j in range(s.scale_planes):
                code = block[s.planes + j].astype(jnp.int32).astype(jnp.float32)
                scales[k, j * s.plane[0] : (j + 1) * s.plane[0]] = jnp.exp2(code * (1.0 / FINE)) * (1.0 / STEPS)
    leaving = []
    for comp in range(s.comps):
        chunk = pl.ds(comp * s.energies, s.energies)
        for plane in range(comp * s.energies, (comp + 1) * s.energies):
            pair = plane // PAIR
            for k, (cell, rows, lanes) in enumerate(places):
                value = blocks[k][plane]
                if k != 0:
                    value = value.astype(jnp.int32).astype(jnp.float32) * scales[k, pair : pair + 1]
                whole_ref[plane, cell, rows, lanes] = value
        leaving.append(pltpu.make_async_copy(whole_ref.at[chunk], whole_hbm.at[chunk], sems.at[comp]))
        leaving[-1].start()
    for copy in leaving:
        copy.wait()


def unpack(s, me, blocks, order):
    shape = (s.planes, s.per_cell, s.rows, s.width)
    return pl.pallas_call(
        functools.partial(unpack_kernel, s, order),
        out_shape=jax.ShapeDtypeStruct(shape, jnp.float32),
        in_specs=[SMEM] + [VMEM] * s.groups,
        out_specs=ANY,
        scratch_shapes=[
            pltpu.VMEM(shape, jnp.float32),
            pltpu.VMEM((s.groups, s.scale_planes * s.plane[0], LANES), jnp.float32),
            pltpu.SemaphoreType.DMA((s.comps,)),
        ],
        compiler_params=PARAMS,
        name="unpack",
    )(me, *[blocks[k] for k in order])


def swap(s, block, k):
    return block if k == 0 else lax.ppermute(block, "energy", [(i, i ^ k) for i in range(s.groups)])


def send_screened(s, cell_map, screened):
    if s.parts == 1:
        return lax.all_to_all(pick_screened(s, cell_map, screened), ("energy", "cell"), 0, 0, tiled=True)
    chosen = jnp.take(screened, cell_map, axis=2).reshape(s.planes, s.cells, s.per_cell, s.held, s.width)
    whole = lax.all_to_all(chosen, "cell", 1, 3, tiled=True)
    cut = whole.reshape(s.planes, s.per_cell, s.parts, s.plane[0], s.tiles, LANES)
    cut = jnp.transpose(cut, (1, 4, 2, 0, 3, 5)).reshape((s.groups, s.planes) + s.plane)
    return lax.all_to_all(cut, "energy", 0, 0, tiled=True)


def per_device(green, screened, cell_map, shift_table, shift_count):
    s = Sizes(green, screened, lax.axis_size("energy"), lax.axis_size("cell"))
    me = lax.axis_index("energy").astype(jnp.int32).reshape(1)
    half = s.groups // 2
    far, near = list(range(half, s.groups)), list(range(half))

    screens = send_screened(s, cell_map, screened)
    greens = [swap(s, block, k) for k, block in enumerate(cut_green(s, me, green))]
    table = shift_table.reshape(s.groups * s.groups, shift_table.shape[2])
    g_near, w_all = stage_near(s, me, screens, greens[:half])
    begun = partial_of(s, me, table, shift_count, g_near, w_all)
    g_far = stage_far(s, me, greens[half:], begun)
    first, later = far[2:], [0] + near[3:] + far[1:2] + near[1:2] + far[:1] + near[2:3]
    sums = {}
    for ks in (first, later):
        for k, block in zip(ks, sigma_of(s, me, table, shift_count, begun, w_all, g_far, ks)):
            sums[k] = swap(s, block, k)
    return unpack(s, me, sums, later + first).reshape(green.shape)


def solution(mesh):
    placed = (
        P(None, "energy", "cell", None, None),
        P(None, "energy", None, "cell", None),
        P(),
        P(),
        P(),
    )
    return jax.shard_map(
        per_device,
        mesh=mesh,
        in_specs=placed,
        out_specs=P(None, "energy", "cell", None, None),
        check_vma=False,
    )
```

```python
import functools

import jax
import jax.numpy as jnp
from jax import lax
from jax.experimental import pallas as pl
from jax.experimental.pallas import tpu as pltpu
from jax.sharding import PartitionSpec as P

SCALE = 0.2
LANES = 128
PAIR = 2
STEPS = 32700.0
FINE = 64.0
TINY = 1e-34
PICKS = 8
SMEM = pl.BlockSpec(memory_space=pltpu.SMEM)
VMEM = pl.BlockSpec(memory_space=pltpu.VMEM)
ANY = pl.BlockSpec(memory_space=pl.ANY)
PARAMS = pltpu.CompilerParams(vmem_limit_bytes=32 * 1024 * 1024)


class Sizes:
    def __init__(self, green, screened, groups, cells):
        self.comps, self.energies, self.per_cell, self.rows, self.width = green.shape
        self.groups, self.cells = groups, cells
        self.tiles = self.width // LANES
        self.slices = groups // self.per_cell
        self.parts = self.slices // self.tiles
        self.held = screened.shape[3]
        self.plane = (self.rows // self.parts, LANES)
        self.planes = self.comps * self.energies
        self.half = groups // 2
        self.held_planes = (self.half + 2) * self.energies
        self.scales = self.planes // PAIR
        self.scale_planes = -(-self.scales // self.plane[0])

    def where(self, index):
        cell, tile, part = index // self.slices, (index // self.parts) % self.tiles, index % self.parts
        return cell, part, pl.ds(pl.multiple_of(tile * LANES, LANES), LANES)


def part_of(s, value, part):
    count = value.shape[0] // s.parts
    chosen = value[:count]
    for other in range(1, s.parts):
        chosen = jnp.where(part == other, value[other * count : (other + 1) * count], chosen)
    return chosen


def pick_kernel(s, map_hbm, screened_hbm, out_hbm, map_ref, screened_ref, out_ref, in_sems, out_sems, map_sem):
    size = s.planes // PICKS
    chunks = [pl.ds(i * size, size) for i in range(PICKS)]
    arriving = [
        pltpu.make_async_copy(screened_hbm.at[chunk], screened_ref.at[chunk], in_sems.at[i])
        for i, chunk in enumerate(chunks)
    ]
    leaving = [
        pltpu.make_async_copy(out_ref.at[:, chunk], out_hbm.at[:, chunk], out_sems.at[i])
        for i, chunk in enumerate(chunks)
    ]
    mapped = pltpu.make_async_copy(map_hbm, map_ref, map_sem)
    mapped.start()
    for copy in arriving:
        copy.start()
    mapped.wait()
    picked = [map_ref[i] for i in range(s.cells * s.per_cell)]
    for chunk in range(PICKS):
        arriving[chunk].wait()
        for plane in range(chunk * size, (chunk + 1) * size):
            for i, cell in enumerate(picked):
                for t in range(s.tiles):
                    target = (i % s.per_cell * s.slices + t) * s.cells + i // s.per_cell
                    out_ref[target, plane] = screened_ref[plane, cell, :, t * LANES : (t + 1) * LANES]
        leaving[chunk].start()
    for copy in leaving:
        copy.wait()


def pick_screened(s, cell_map, screened):
    out = jax.ShapeDtypeStruct((s.groups * s.cells, s.planes, s.held, LANES), screened.dtype)
    flat = screened.reshape((s.planes,) + screened.shape[2:])
    return pl.pallas_call(
        functools.partial(pick_kernel, s),
        out_shape=out,
        in_specs=[ANY, ANY],
        out_specs=ANY,
        scratch_shapes=[
            pltpu.SMEM(cell_map.shape, jnp.int32),
            pltpu.VMEM(flat.shape, flat.dtype),
            pltpu.VMEM(out.shape, out.dtype),
            pltpu.SemaphoreType.DMA((PICKS,)),
            pltpu.SemaphoreType.DMA((PICKS,)),
            pltpu.SemaphoreType.DMA(()),
        ],
        compiler_params=pltpu.CompilerParams(vmem_limit_bytes=60 * 1024 * 1024),
        name="pick_screened",
    )(cell_map, flat)


def cut_kernel(s, me_ref, green_ref, *greens):
    me = me_ref[0]
    places = [s.where(me ^ k) for k in range(s.groups)]

    for plane in range(s.planes):
        for k, (cell, part, lanes) in enumerate(places):
            value = green_ref[plane, cell, :, lanes]
            if s.parts > 1:
                value = part_of(s, value.astype(jnp.float32), part).astype(greens[k].dtype)
            greens[k][plane] = value


def cut_green(s, me, green):
    return pl.pallas_call(
        functools.partial(cut_kernel, s),
        out_shape=[jax.ShapeDtypeStruct((s.planes,) + s.plane, green.dtype)] * s.groups,
        in_specs=[SMEM, VMEM],
        out_specs=[VMEM] * s.groups,
        compiler_params=PARAMS,
        name="cut_green",
    )(me, green.reshape((s.planes,) + green.shape[2:]))


def held(s):
    return jax.ShapeDtypeStruct((s.comps * s.held_planes,) + s.plane, jnp.float32)


def stage_green(s, me, first, blocks, g_half):
    zero = jnp.zeros(s.plane, jnp.float32)
    spots = [((me ^ (first + k)) % s.half + 1) * s.energies for k in range(s.half)]

    @pl.loop(0, s.energies)
    def _(j):
        for comp in range(s.comps):
            base = comp * s.held_planes + j
            g_half[base] = zero
            g_half[base + (s.half + 1) * s.energies] = zero
            for spot, block in zip(spots, blocks):
                g_half[base + spot] = block[comp * s.energies + j].astype(jnp.float32)


def stage_near_kernel(s, me_ref, screens_ref, *refs):
    g_half, w_all = refs[-2:]
    stage_green(s, me_ref[0], 0, refs[:-2], g_half)

    @pl.loop(0, s.planes)
    def _(plane):
        for source in range(s.groups):
            if s.parts > 1:
                w_all[source, plane] = screens_ref[source, plane].astype(jnp.float32)
                continue
            for c in range(s.cells):
                piece = screens_ref[source * s.cells + c, plane].astype(jnp.float32)
                w_all[source, plane, c * s.held : (c + 1) * s.held, :] = piece


def stage_near(s, me, screens, greens):
    return pl.pallas_call(
        functools.partial(stage_near_kernel, s),
        out_shape=[held(s), jax.ShapeDtypeStruct((s.groups, s.planes) + s.plane, jnp.float32)],
        in_specs=[SMEM] + [VMEM] * (len(greens) + 1),
        out_specs=[VMEM] * 2,
        compiler_params=PARAMS,
        name="stage_near",
    )(me, screens, *greens)


def stage_far_kernel(s, me_ref, after_ref, *refs):
    stage_green(s, me_ref[0], s.groups // 2, refs[:-1], refs[-1])


def stage_far(s, me, greens, after):
    return pl.pallas_call(
        functools.partial(stage_far_kernel, s),
        out_shape=held(s),
        in_specs=[SMEM, ANY] + [VMEM] * len(greens),
        out_specs=VMEM,
        compiler_params=PARAMS,
        name="stage_far",
    )(me, after, *greens)


def add_terms(s, slots, side, group, kind, table_ref, g_half, w_all, sums):
    low = side * s.half
    real, imag = 2 * kind, 2 * kind + 1

    def turn(source, sums):
        sums = list(sums)
        for slot in range(slots):
            asked = table_ref[group * s.groups + source, slot]
            shift = jnp.maximum(asked, 0)
            live = jnp.where(asked >= 0, 1.0, 0.0).astype(jnp.float32)
            start = (group - source - low + 1) * s.energies - shift
            w_real = w_all[source, real * s.energies + shift] * live
            w_imag = w_all[source, imag * s.energies + shift] * live
            for j in range(s.energies):
                g_real = g_half[real * s.held_planes + start + j]
                g_imag = g_half[imag * s.held_planes + start + j]
                sums[j] = sums[j] - (g_real * w_imag + g_imag * w_real)
                sums[s.energies + j] = sums[s.energies + j] + (g_real * w_real - g_imag * w_imag)
        return tuple(sums)

    first = jnp.maximum(group - low - s.half, 0)
    return lax.fori_loop(first, jnp.maximum(group - low + 1, first), turn, tuple(sums))


def partial_kernel(s, slots, me_ref, table_ref, g_half, w_all, out_ref):
    me = me_ref[0]

    @pl.loop(0, 2 * s.groups)
    def _(at):
        k, kind = at // 2, at % 2
        zeros = [jnp.zeros(s.plane, jnp.float32) for _ in range(2 * s.energies)]
        sums = add_terms(s, slots, me // s.half, me ^ k, kind, table_ref, g_half, w_all, zeros)
        for j, total in enumerate(sums):
            out_ref[k, kind * 2 * s.energies + j] = total


def partial_of(s, me, table, g_half, w_all):
    return pl.pallas_call(
        functools.partial(partial_kernel, s, table.shape[1]),
        out_shape=jax.ShapeDtypeStruct((s.groups, s.planes) + s.plane, jnp.float32),
        in_specs=[SMEM] * 2 + [VMEM] * 2,
        out_specs=VMEM,
        compiler_params=PARAMS,
        name="partial",
    )(me, table, g_half, w_all)


def sigma_kernel(s, slots, ks, me_ref, table_ref, begun, w_all, g_far, *outs):
    me = me_ref[0]
    side = me // s.half
    row = lax.broadcasted_iota(jnp.int32, s.plane, 0)
    for at, k in enumerate(ks):

        def turn(kind, codes):
            codes = list(codes)
            first = kind * 2 * s.energies
            sums = [begun[k, first + j] for j in range(2 * s.energies)]
            sums = add_terms(s, slots, 1 - side, me ^ k, kind, table_ref, g_far, w_all, sums)
            sums = [total * SCALE for total in sums]
            if k == 0:
                for j, total in enumerate(sums):
                    outs[at][first + j] = total
                return tuple(codes)
            for low in range(0, 2 * s.energies, PAIR):
                pair = sums[low : low + PAIR]
                largest = functools.reduce(jnp.maximum, [jnp.abs(total) for total in pair])
                largest = jnp.maximum(jnp.max(largest, axis=0, keepdims=True), TINY)
                code = jnp.ceil(jnp.log2(largest) * FINE)
                inverse = jnp.exp2(code * (-1.0 / FINE)) * STEPS
                where = (first + low) // PAIR
                for i in range(s.scale_planes):
                    codes[i] = jnp.where(row + i * s.plane[0] == where, code, codes[i])
                for j, total in enumerate(pair):
                    coded = jnp.round(total * inverse).astype(jnp.int32)
                    outs[at][first + low + j] = coded.astype(jnp.int16)
            return tuple(codes)

        codes = lax.fori_loop(0, 2, turn, tuple(jnp.zeros(s.plane, jnp.float32) for _ in range(s.scale_planes)))
        if k != 0:
            for j in range(s.scale_planes):
                outs[at][s.planes + j] = codes[j].astype(jnp.int32).astype(jnp.int16)


def sigma_of(s, me, table, begun, w_all, g_far, ks):
    own = jax.ShapeDtypeStruct((s.planes,) + s.plane, jnp.float32)
    coded = jax.ShapeDtypeStruct((s.planes + s.scale_planes,) + s.plane, jnp.int16)
    return pl.pallas_call(
        functools.partial(sigma_kernel, s, table.shape[1], ks),
        out_shape=[own if k == 0 else coded for k in ks],
        in_specs=[SMEM] * 2 + [VMEM] * 3,
        out_specs=[VMEM] * len(ks),
        compiler_params=PARAMS,
        name="sigma",
    )(me, table, begun, w_all, g_far)


def unpack_kernel(s, order, me_ref, *refs):
    at = dict(zip(order, refs))
    blocks = [at[k] for k in range(s.groups)]
    whole_hbm, whole_ref, scales, sems = refs[s.groups :]
    me = me_ref[0]
    places = []
    for k, block in enumerate(blocks):
        cell, part, lanes = s.where(me ^ k)
        rows = slice(None) if s.parts == 1 else pl.ds(pl.multiple_of(part * s.plane[0], s.plane[0]), s.plane[0])
        places.append((cell, rows, lanes))
        if k != 0:
            for j in range(s.scale_planes):
                code = block[s.planes + j].astype(jnp.int32).astype(jnp.float32)
                scales[k, j * s.plane[0] : (j + 1) * s.plane[0]] = jnp.exp2(code * (1.0 / FINE)) * (1.0 / STEPS)
    leaving = []
    for comp in range(s.comps):
        chunk = pl.ds(comp * s.energies, s.energies)
        for plane in range(comp * s.energies, (comp + 1) * s.energies):
            pair = plane // PAIR
            for k, (cell, rows, lanes) in enumerate(places):
                value = blocks[k][plane]
                if k != 0:
                    value = value.astype(jnp.int32).astype(jnp.float32) * scales[k, pair : pair + 1]
                whole_ref[plane, cell, rows, lanes] = value
        leaving.append(pltpu.make_async_copy(whole_ref.at[chunk], whole_hbm.at[chunk], sems.at[comp]))
        leaving[-1].start()
    for copy in leaving:
        copy.wait()


def unpack(s, me, blocks, order):
    shape = (s.planes, s.per_cell, s.rows, s.width)
    return pl.pallas_call(
        functools.partial(unpack_kernel, s, order),
        out_shape=jax.ShapeDtypeStruct(shape, jnp.float32),
        in_specs=[SMEM] + [VMEM] * s.groups,
        out_specs=ANY,
        scratch_shapes=[
            pltpu.VMEM(shape, jnp.float32),
            pltpu.VMEM((s.groups, s.scale_planes * s.plane[0], LANES), jnp.float32),
            pltpu.SemaphoreType.DMA((s.comps,)),
        ],
        compiler_params=PARAMS,
        name="unpack",
    )(me, *[blocks[k] for k in order])


def swap(s, block, k):
    return block if k == 0 else lax.ppermute(block, "energy", [(i, i ^ k) for i in range(s.groups)])


def send_screened(s, cell_map, screened):
    if s.parts == 1:
        return lax.all_to_all(pick_screened(s, cell_map, screened), ("energy", "cell"), 0, 0, tiled=True)
    chosen = jnp.take(screened, cell_map, axis=2).reshape(s.planes, s.cells, s.per_cell, s.held, s.width)
    whole = lax.all_to_all(chosen, "cell", 1, 3, tiled=True)
    cut = whole.reshape(s.planes, s.per_cell, s.parts, s.plane[0], s.tiles, LANES)
    cut = jnp.transpose(cut, (1, 4, 2, 0, 3, 5)).reshape((s.groups, s.planes) + s.plane)
    return lax.all_to_all(cut, "energy", 0, 0, tiled=True)


def per_device(green, screened, cell_map, shift_table, shift_count):
    s = Sizes(green, screened, lax.axis_size("energy"), lax.axis_size("cell"))
    me = lax.axis_index("energy").astype(jnp.int32).reshape(1)
    half = s.groups // 2
    far, near = list(range(half, s.groups)), list(range(half))

    screens = send_screened(s, cell_map, screened)
    greens = [swap(s, block, k) for k, block in enumerate(cut_green(s, me, green))]
    slots = jnp.arange(shift_table.shape[2], dtype=jnp.int32)
    table = jnp.where(slots < shift_count[:, :, None], jnp.clip(shift_table, 0, s.energies - 1), -1)
    table = table.reshape(s.groups * s.groups, shift_table.shape[2])
    g_near, w_all = stage_near(s, me, screens, greens[:half])
    begun = partial_of(s, me, table, g_near, w_all)
    g_far = stage_far(s, me, greens[half:], begun)
    first, later = far[2:], [0] + near[2:3] + near[3:] + near[1:2] + far[:1] + far[1:2]
    sums = {}
    for ks in (first, later):
        for k, block in zip(ks, sigma_of(s, me, table, begun, w_all, g_far, ks)):
            sums[k] = swap(s, block, k)
    return unpack(s, me, sums, later + first).reshape(green.shape)


def solution(mesh):
    placed = (
        P(None, "energy", "cell", None, None),
        P(None, "energy", None, "cell", None),
        P(),
        P(),
        P(),
    )
    return jax.shard_map(
        per_device,
        mesh=mesh,
        in_specs=placed,
        out_specs=P(None, "energy", "cell", None, None),
        check_vma=False,
    )
```

```python
import functools

import jax
import jax.numpy as jnp
from jax import lax
from jax.experimental import pallas as pl
from jax.experimental.pallas import tpu as pltpu
from jax.sharding import PartitionSpec as P

SCALE = 0.2
LANES = 128
PAIR = 4
STEPS = 32700.0
STRIP = 8
FINE = 64.0
TINY = 1e-34
PICKS = 8
SMEM = pl.BlockSpec(memory_space=pltpu.SMEM)
VMEM = pl.BlockSpec(memory_space=pltpu.VMEM)
ANY = pl.BlockSpec(memory_space=pl.ANY)
PARAMS = pltpu.CompilerParams(vmem_limit_bytes=32 * 1024 * 1024)


class Sizes:
    def __init__(self, green, screened, groups, cells):
        self.comps, self.energies, self.per_cell, self.rows, self.width = green.shape
        self.groups, self.cells = groups, cells
        self.tiles = self.width // LANES
        self.slices = groups // self.per_cell
        self.parts = self.slices // self.tiles
        self.held = screened.shape[3]
        self.plane = (self.rows // self.parts, LANES)
        self.planes = self.comps * self.energies
        self.half = groups // 2
        self.held_planes = (self.half + 2) * self.energies
        self.scales = self.planes // PAIR
        self.strips = self.plane[0] // STRIP
        self.scale_strips = -(-self.scales // STRIP)

    def where(self, index):
        cell, tile, part = index // self.slices, (index // self.parts) % self.tiles, index % self.parts
        return cell, part, pl.ds(pl.multiple_of(tile * LANES, LANES), LANES)


def part_of(s, value, part):
    count = value.shape[0] // s.parts
    chosen = value[:count]
    for other in range(1, s.parts):
        chosen = jnp.where(part == other, value[other * count : (other + 1) * count], chosen)
    return chosen


def pick_kernel(s, map_hbm, screened_hbm, out_hbm, map_ref, screened_ref, out_ref, in_sems, out_sems, map_sem):
    size = s.planes // PICKS
    chunks = [pl.ds(i * size, size) for i in range(PICKS)]
    arriving = [
        pltpu.make_async_copy(screened_hbm.at[chunk], screened_ref.at[chunk], in_sems.at[i])
        for i, chunk in enumerate(chunks)
    ]
    leaving = [
        pltpu.make_async_copy(out_ref.at[:, chunk], out_hbm.at[:, chunk], out_sems.at[i])
        for i, chunk in enumerate(chunks)
    ]
    mapped = pltpu.make_async_copy(map_hbm, map_ref, map_sem)
    mapped.start()
    for copy in arriving:
        copy.start()
    mapped.wait()
    picked = [map_ref[i] for i in range(s.cells * s.per_cell)]
    for chunk in range(PICKS):
        arriving[chunk].wait()
        for plane in range(chunk * size, (chunk + 1) * size):
            for i, cell in enumerate(picked):
                for t in range(s.tiles):
                    target = (i % s.per_cell * s.slices + t) * s.cells + i // s.per_cell
                    out_ref[target, plane] = screened_ref[plane, cell, :, t * LANES : (t + 1) * LANES]
        leaving[chunk].start()
    for copy in leaving:
        copy.wait()


def pick_screened(s, cell_map, screened):
    out = jax.ShapeDtypeStruct((s.groups * s.cells, s.planes, s.held, LANES), screened.dtype)
    flat = screened.reshape((s.planes,) + screened.shape[2:])
    return pl.pallas_call(
        functools.partial(pick_kernel, s),
        out_shape=out,
        in_specs=[ANY, ANY],
        out_specs=ANY,
        scratch_shapes=[
            pltpu.SMEM(cell_map.shape, jnp.int32),
            pltpu.VMEM(flat.shape, flat.dtype),
            pltpu.VMEM(out.shape, out.dtype),
            pltpu.SemaphoreType.DMA((PICKS,)),
            pltpu.SemaphoreType.DMA((PICKS,)),
            pltpu.SemaphoreType.DMA(()),
        ],
        compiler_params=pltpu.CompilerParams(vmem_limit_bytes=60 * 1024 * 1024),
        name="pick_screened",
    )(cell_map, flat)


def cut_kernel(s, me_ref, green_ref, *greens):
    me = me_ref[0]
    places = [s.where(me ^ k) for k in range(s.groups)]

    for plane in range(s.planes):
        for k, (cell, part, lanes) in enumerate(places):
            value = green_ref[plane, cell, :, lanes]
            if s.parts > 1:
                value = part_of(s, value.astype(jnp.float32), part).astype(greens[k].dtype)
            greens[k][plane] = value


def cut_green(s, me, green):
    return pl.pallas_call(
        functools.partial(cut_kernel, s),
        out_shape=[jax.ShapeDtypeStruct((s.planes,) + s.plane, green.dtype)] * s.groups,
        in_specs=[SMEM, VMEM],
        out_specs=[VMEM] * s.groups,
        compiler_params=PARAMS,
        name="cut_green",
    )(me, green.reshape((s.planes,) + green.shape[2:]))


def held(s):
    return jax.ShapeDtypeStruct((s.comps * s.held_planes,) + s.plane, jnp.float32)


def stage_green(s, me, first, blocks, g_half):
    zero = jnp.zeros(s.plane, jnp.float32)
    spots = [((me ^ (first + k)) % s.half + 1) * s.energies for k in range(s.half)]

    @pl.loop(0, s.energies)
    def _(j):
        for comp in range(s.comps):
            base = comp * s.held_planes + j
            g_half[base] = zero
            g_half[base + (s.half + 1) * s.energies] = zero
            for spot, block in zip(spots, blocks):
                g_half[base + spot] = block[comp * s.energies + j].astype(jnp.float32)


def stage_near_kernel(s, me_ref, screens_ref, *refs):
    g_half, w_all = refs[-2:]
    stage_green(s, me_ref[0], 0, refs[:-2], g_half)

    @pl.loop(0, s.planes)
    def _(plane):
        for source in range(s.groups):
            if s.parts > 1:
                w_all[source, plane] = screens_ref[source, plane].astype(jnp.float32)
                continue
            for c in range(s.cells):
                piece = screens_ref[source * s.cells + c, plane].astype(jnp.float32)
                w_all[source, plane, c * s.held : (c + 1) * s.held, :] = piece


def stage_near(s, me, screens, greens):
    return pl.pallas_call(
        functools.partial(stage_near_kernel, s),
        out_shape=[held(s), jax.ShapeDtypeStruct((s.groups, s.planes) + s.plane, jnp.float32)],
        in_specs=[SMEM] + [VMEM] * (len(greens) + 1),
        out_specs=[VMEM] * 2,
        compiler_params=PARAMS,
        name="stage_near",
    )(me, screens, *greens)


def stage_far_kernel(s, me_ref, after_ref, *refs):
    stage_green(s, me_ref[0], s.groups // 2, refs[:-1], refs[-1])


def stage_far(s, me, greens, after):
    return pl.pallas_call(
        functools.partial(stage_far_kernel, s),
        out_shape=held(s),
        in_specs=[SMEM, ANY] + [VMEM] * len(greens),
        out_specs=VMEM,
        compiler_params=PARAMS,
        name="stage_far",
    )(me, after, *greens)


def add_terms(s, slots, side, group, kind, table_ref, g_half, w_all, sums):
    low = side * s.half
    real, imag = 2 * kind, 2 * kind + 1

    def turn(source, sums):
        sums = list(sums)
        for slot in range(slots):
            asked = table_ref[group * s.groups + source, slot]
            shift = jnp.maximum(asked, 0)
            live = jnp.where(asked >= 0, 1.0, 0.0).astype(jnp.float32)
            start = (group - source - low + 1) * s.energies - shift
            w_real = w_all[source, real * s.energies + shift] * live
            w_imag = w_all[source, imag * s.energies + shift] * live
            for j in range(s.energies):
                g_real = g_half[real * s.held_planes + start + j]
                g_imag = g_half[imag * s.held_planes + start + j]
                sums[j] = sums[j] - (g_real * w_imag + g_imag * w_real)
                sums[s.energies + j] = sums[s.energies + j] + (g_real * w_real - g_imag * w_imag)
        return tuple(sums)

    first = jnp.maximum(group - low - s.half, 0)
    return lax.fori_loop(first, jnp.maximum(group - low + 1, first), turn, tuple(sums))


def partial_kernel(s, slots, me_ref, table_ref, g_half, w_all, out_ref):
    me = me_ref[0]

    @pl.loop(0, 2 * s.groups)
    def _(at):
        k, kind = at // 2, at % 2
        zeros = [jnp.zeros(s.plane, jnp.float32) for _ in range(2 * s.energies)]
        sums = add_terms(s, slots, me // s.half, me ^ k, kind, table_ref, g_half, w_all, zeros)
        for j, total in enumerate(sums):
            out_ref[k, kind * 2 * s.energies + j] = total


def partial_of(s, me, table, g_half, w_all):
    return pl.pallas_call(
        functools.partial(partial_kernel, s, table.shape[1]),
        out_shape=jax.ShapeDtypeStruct((s.groups, s.planes) + s.plane, jnp.float32),
        in_specs=[SMEM] * 2 + [VMEM] * 2,
        out_specs=VMEM,
        compiler_params=PARAMS,
        name="partial",
    )(me, table, g_half, w_all)


def sigma_kernel(s, slots, ks, me_ref, table_ref, begun, w_all, g_far, *outs):
    me = me_ref[0]
    side = me // s.half
    row = lax.broadcasted_iota(jnp.int32, (STRIP, LANES), 0)
    for at, k in enumerate(ks):

        def turn(kind, codes):
            codes = list(codes)
            first = kind * 2 * s.energies
            sums = [begun[k, first + j] for j in range(2 * s.energies)]
            sums = add_terms(s, slots, 1 - side, me ^ k, kind, table_ref, g_far, w_all, sums)
            sums = [total * SCALE for total in sums]
            if k == 0:
                for j, total in enumerate(sums):
                    outs[at][first + j] = total
                return tuple(codes)
            for low in range(0, 2 * s.energies, PAIR):
                pair = sums[low : low + PAIR]
                largest = functools.reduce(jnp.maximum, [jnp.abs(total) for total in pair])
                largest = jnp.maximum(jnp.max(largest, axis=0, keepdims=True), TINY)
                code = jnp.ceil(jnp.log2(largest) * FINE)
                inverse = jnp.exp2(code * (-1.0 / FINE)) * STEPS
                where = (first + low) // PAIR
                for i in range(s.scale_strips):
                    codes[i] = jnp.where(row + i * STRIP == where, code, codes[i])
                for j, total in enumerate(pair):
                    coded = jnp.round(total * inverse).astype(jnp.int32)
                    for i in range(s.strips):
                        strip = coded[i * STRIP : (i + 1) * STRIP].astype(jnp.int16)
                        outs[at][(first + low + j) * s.strips + i] = strip
            return tuple(codes)

        codes = lax.fori_loop(0, 2, turn, tuple(jnp.zeros((STRIP, LANES), jnp.float32) for _ in range(s.scale_strips)))
        if k != 0:
            for j in range(s.scale_strips):
                outs[at][s.planes * s.strips + j] = codes[j].astype(jnp.int32).astype(jnp.int16)


def sigma_of(s, me, table, begun, w_all, g_far, ks):
    own = jax.ShapeDtypeStruct((s.planes,) + s.plane, jnp.float32)
    coded = jax.ShapeDtypeStruct((s.planes * s.strips + s.scale_strips, STRIP, LANES), jnp.int16)
    return pl.pallas_call(
        functools.partial(sigma_kernel, s, table.shape[1], ks),
        out_shape=[own if k == 0 else coded for k in ks],
        in_specs=[SMEM] * 2 + [VMEM] * 3,
        out_specs=[VMEM] * len(ks),
        compiler_params=PARAMS,
        name="sigma",
    )(me, table, begun, w_all, g_far)


def unpack_kernel(s, order, me_ref, *refs):
    at = dict(zip(order, refs))
    blocks = [at[k] for k in range(s.groups)]
    whole_hbm, whole_ref, scales, sems = refs[s.groups :]
    me = me_ref[0]
    places = []
    for k, block in enumerate(blocks):
        cell, part, lanes = s.where(me ^ k)
        rows = slice(None) if s.parts == 1 else pl.ds(pl.multiple_of(part * s.plane[0], s.plane[0]), s.plane[0])
        places.append((cell, rows, lanes))
        if k != 0:
            for j in range(s.scale_strips):
                code = block[s.planes * s.strips + j].astype(jnp.int32).astype(jnp.float32)
                scales[k, j * STRIP : (j + 1) * STRIP] = jnp.exp2(code * (1.0 / FINE)) * (1.0 / STEPS)
    leaving = []
    for comp in range(s.comps):
        chunk = pl.ds(comp * s.energies, s.energies)
        for plane in range(comp * s.energies, (comp + 1) * s.energies):
            pair = plane // PAIR
            for k, (cell, rows, lanes) in enumerate(places):
                if k == 0:
                    value = blocks[0][plane]
                else:
                    strips = [blocks[k][plane * s.strips + i].astype(jnp.int32) for i in range(s.strips)]
                    value = jnp.concatenate(strips, axis=0).astype(jnp.float32) * scales[k, pair : pair + 1]
                whole_ref[plane, cell, rows, lanes] = value
        leaving.append(pltpu.make_async_copy(whole_ref.at[chunk], whole_hbm.at[chunk], sems.at[comp]))
        leaving[-1].start()
    for copy in leaving:
        copy.wait()


def unpack(s, me, blocks, order):
    shape = (s.planes, s.per_cell, s.rows, s.width)
    return pl.pallas_call(
        functools.partial(unpack_kernel, s, order),
        out_shape=jax.ShapeDtypeStruct(shape, jnp.float32),
        in_specs=[SMEM] + [VMEM] * s.groups,
        out_specs=ANY,
        scratch_shapes=[
            pltpu.VMEM(shape, jnp.float32),
            pltpu.VMEM((s.groups, s.scale_strips * STRIP, LANES), jnp.float32),
            pltpu.SemaphoreType.DMA((s.comps,)),
        ],
        compiler_params=PARAMS,
        name="unpack",
    )(me, *[blocks[k] for k in order])


def swap(s, block, k):
    return block if k == 0 else lax.ppermute(block, "energy", [(i, i ^ k) for i in range(s.groups)])


def send_screened(s, cell_map, screened):
    if s.parts == 1:
        return lax.all_to_all(pick_screened(s, cell_map, screened), ("energy", "cell"), 0, 0, tiled=True)
    chosen = jnp.take(screened, cell_map, axis=2).reshape(s.planes, s.cells, s.per_cell, s.held, s.width)
    whole = lax.all_to_all(chosen, "cell", 1, 3, tiled=True)
    cut = whole.reshape(s.planes, s.per_cell, s.parts, s.plane[0], s.tiles, LANES)
    cut = jnp.transpose(cut, (1, 4, 2, 0, 3, 5)).reshape((s.groups, s.planes) + s.plane)
    return lax.all_to_all(cut, "energy", 0, 0, tiled=True)


def per_device(green, screened, cell_map, shift_table, shift_count):
    s = Sizes(green, screened, lax.axis_size("energy"), lax.axis_size("cell"))
    me = lax.axis_index("energy").astype(jnp.int32).reshape(1)
    half = s.groups // 2
    far, near = list(range(half, s.groups)), list(range(half))

    screens = send_screened(s, cell_map, screened)
    greens = [swap(s, block, k) for k, block in enumerate(cut_green(s, me, green))]
    slots = jnp.arange(shift_table.shape[2], dtype=jnp.int32)
    table = jnp.where(slots < shift_count[:, :, None], jnp.clip(shift_table, 0, s.energies - 1), -1)
    table = table.reshape(s.groups * s.groups, shift_table.shape[2])
    g_near, w_all = stage_near(s, me, screens, greens[:half])
    begun = partial_of(s, me, table, g_near, w_all)
    g_far = stage_far(s, me, greens[half:], begun)
    first, later = far[2:], [0] + near[2:3] + near[3:] + near[1:2] + far[:1] + far[1:2]
    sums = {}
    for ks in (first, later):
        for k, block in zip(ks, sigma_of(s, me, table, begun, w_all, g_far, ks)):
            sums[k] = swap(s, block, k)
    return unpack(s, me, sums, later + first).reshape(green.shape)


def solution(mesh):
    placed = (
        P(None, "energy", "cell", None, None),
        P(None, "energy", None, "cell", None),
        P(),
        P(),
        P(),
    )
    return jax.shard_map(
        per_device,
        mesh=mesh,
        in_specs=placed,
        out_specs=P(None, "energy", "cell", None, None),
        check_vma=False,
    )
```

```python
import functools

import jax
import jax.numpy as jnp
from jax import lax
from jax.experimental import pallas as pl
from jax.experimental.pallas import tpu as pltpu
from jax.sharding import PartitionSpec as P

SCALE = 0.2
LANES = 128
PAIR = 4
STEPS = 32700.0
STRIP = 8
FINE = 64.0
TINY = 1e-34
PICKS = 8
SMEM = pl.BlockSpec(memory_space=pltpu.SMEM)
VMEM = pl.BlockSpec(memory_space=pltpu.VMEM)
ANY = pl.BlockSpec(memory_space=pl.ANY)
PARAMS = pltpu.CompilerParams(vmem_limit_bytes=32 * 1024 * 1024)


class Sizes:
    def __init__(self, green, screened, groups, cells):
        self.comps, self.energies, self.per_cell, self.rows, self.width = green.shape
        self.groups, self.cells = groups, cells
        self.tiles = self.width // LANES
        self.slices = groups // self.per_cell
        self.parts = self.slices // self.tiles
        self.held = screened.shape[3]
        self.plane = (self.rows // self.parts, LANES)
        self.planes = self.comps * self.energies
        self.half = groups // 2
        self.held_planes = (self.half + 2) * self.energies
        self.scales = self.planes // PAIR
        self.strips = self.plane[0] // STRIP
        self.scale_strips = -(-self.scales // STRIP)

    def where(self, index):
        cell, tile, part = index // self.slices, (index // self.parts) % self.tiles, index % self.parts
        return cell, part, pl.ds(pl.multiple_of(tile * LANES, LANES), LANES)


def part_of(s, value, part):
    count = value.shape[0] // s.parts
    chosen = value[:count]
    for other in range(1, s.parts):
        chosen = jnp.where(part == other, value[other * count : (other + 1) * count], chosen)
    return chosen


def pick_kernel(s, map_hbm, screened_hbm, out_hbm, map_ref, screened_ref, out_ref, in_sems, out_sems, map_sem):
    size = s.planes // PICKS
    chunks = [pl.ds(i * size, size) for i in range(PICKS)]
    arriving = [
        pltpu.make_async_copy(screened_hbm.at[chunk], screened_ref.at[chunk], in_sems.at[i])
        for i, chunk in enumerate(chunks)
    ]
    leaving = [
        pltpu.make_async_copy(out_ref.at[:, chunk], out_hbm.at[:, chunk], out_sems.at[i])
        for i, chunk in enumerate(chunks)
    ]
    mapped = pltpu.make_async_copy(map_hbm, map_ref, map_sem)
    mapped.start()
    for copy in arriving:
        copy.start()
    mapped.wait()
    picked = [map_ref[i] for i in range(s.cells * s.per_cell)]
    for chunk in range(PICKS):
        arriving[chunk].wait()
        for plane in range(chunk * size, (chunk + 1) * size):
            for i, cell in enumerate(picked):
                for t in range(s.tiles):
                    target = (i % s.per_cell * s.slices + t) * s.cells + i // s.per_cell
                    out_ref[target, plane] = screened_ref[plane, cell, :, t * LANES : (t + 1) * LANES]
        leaving[chunk].start()
    for copy in leaving:
        copy.wait()


def pick_screened(s, cell_map, screened):
    out = jax.ShapeDtypeStruct((s.groups * s.cells, s.planes, s.held, LANES), screened.dtype)
    flat = screened.reshape((s.planes,) + screened.shape[2:])
    return pl.pallas_call(
        functools.partial(pick_kernel, s),
        out_shape=out,
        in_specs=[ANY, ANY],
        out_specs=ANY,
        scratch_shapes=[
            pltpu.SMEM(cell_map.shape, jnp.int32),
            pltpu.VMEM(flat.shape, flat.dtype),
            pltpu.VMEM(out.shape, out.dtype),
            pltpu.SemaphoreType.DMA((PICKS,)),
            pltpu.SemaphoreType.DMA((PICKS,)),
            pltpu.SemaphoreType.DMA(()),
        ],
        compiler_params=pltpu.CompilerParams(vmem_limit_bytes=60 * 1024 * 1024),
        name="pick_screened",
    )(cell_map, flat)


def cut_kernel(s, me_ref, green_ref, *greens):
    me = me_ref[0]
    places = [s.where(me ^ k) for k in range(s.groups)]

    for plane in range(s.planes):
        for k, (cell, part, lanes) in enumerate(places):
            value = green_ref[plane, cell, :, lanes]
            if s.parts > 1:
                value = part_of(s, value.astype(jnp.float32), part).astype(greens[k].dtype)
            greens[k][plane] = value


def cut_green(s, me, green):
    return pl.pallas_call(
        functools.partial(cut_kernel, s),
        out_shape=[jax.ShapeDtypeStruct((s.planes,) + s.plane, green.dtype)] * s.groups,
        in_specs=[SMEM, VMEM],
        out_specs=[VMEM] * s.groups,
        compiler_params=PARAMS,
        name="cut_green",
    )(me, green.reshape((s.planes,) + green.shape[2:]))


def held(s):
    return jax.ShapeDtypeStruct((s.comps * s.held_planes,) + s.plane, jnp.float32)


def stage_green(s, me, first, blocks, g_half):
    zero = jnp.zeros(s.plane, jnp.float32)
    spots = [((me ^ (first + k)) % s.half + 1) * s.energies for k in range(s.half)]

    @pl.loop(0, s.energies)
    def _(j):
        for comp in range(s.comps):
            base = comp * s.held_planes + j
            g_half[base] = zero
            g_half[base + (s.half + 1) * s.energies] = zero
            for spot, block in zip(spots, blocks):
                g_half[base + spot] = block[comp * s.energies + j].astype(jnp.float32)


def stage_near_kernel(s, me_ref, screens_ref, *refs):
    g_half, w_all = refs[-2:]
    stage_green(s, me_ref[0], 0, refs[:-2], g_half)

    for source in range(s.groups):
        w_all[source, s.planes] = jnp.zeros(s.plane, jnp.float32)

    @pl.loop(0, s.planes)
    def _(plane):
        for source in range(s.groups):
            if s.parts > 1:
                w_all[source, plane] = screens_ref[source, plane].astype(jnp.float32) * SCALE
                continue
            for c in range(s.cells):
                piece = screens_ref[source * s.cells + c, plane].astype(jnp.float32) * SCALE
                w_all[source, plane, c * s.held : (c + 1) * s.held, :] = piece


def stage_near(s, me, screens, greens):
    return pl.pallas_call(
        functools.partial(stage_near_kernel, s),
        out_shape=[held(s), jax.ShapeDtypeStruct((s.groups, s.planes + 1) + s.plane, jnp.float32)],
        in_specs=[SMEM] + [VMEM] * (len(greens) + 1),
        out_specs=[VMEM] * 2,
        compiler_params=PARAMS,
        name="stage_near",
    )(me, screens, *greens)


def stage_far_kernel(s, me_ref, after_ref, *refs):
    stage_green(s, me_ref[0], s.groups // 2, refs[:-1], refs[-1])


def stage_far(s, me, greens, after):
    return pl.pallas_call(
        functools.partial(stage_far_kernel, s),
        out_shape=held(s),
        in_specs=[SMEM, ANY] + [VMEM] * len(greens),
        out_specs=VMEM,
        compiler_params=PARAMS,
        name="stage_far",
    )(me, after, *greens)


def add_terms(s, slots, side, group, kind, table_ref, g_half, w_all, sums):
    low = side * s.half
    real, imag = 2 * kind, 2 * kind + 1

    def turn(source, sums):
        sums = list(sums)
        for slot in range(slots):
            asked = table_ref[group * s.groups + source, slot]
            shift = jnp.maximum(asked, 0)
            dead = asked < 0
            start = (group - source - low + 1) * s.energies - shift
            w_real = w_all[source, jnp.where(dead, s.planes, real * s.energies + shift)]
            w_imag = w_all[source, jnp.where(dead, s.planes, imag * s.energies + shift)]
            for j in range(s.energies):
                g_real = g_half[real * s.held_planes + start + j]
                g_imag = g_half[imag * s.held_planes + start + j]
                sums[j] = sums[j] - (g_real * w_imag + g_imag * w_real)
                sums[s.energies + j] = sums[s.energies + j] + (g_real * w_real - g_imag * w_imag)
        return tuple(sums)

    first = jnp.maximum(group - low - s.half, 0)
    return lax.fori_loop(first, jnp.maximum(group - low + 1, first), turn, tuple(sums))


def partial_kernel(s, slots, me_ref, table_ref, g_half, w_all, out_ref):
    me = me_ref[0]

    @pl.loop(0, 2 * s.groups)
    def _(at):
        k, kind = at // 2, at % 2
        zeros = [jnp.zeros(s.plane, jnp.float32) for _ in range(2 * s.energies)]
        sums = add_terms(s, slots, me // s.half, me ^ k, kind, table_ref, g_half, w_all, zeros)
        for j, total in enumerate(sums):
            out_ref[k, kind * 2 * s.energies + j] = total


def partial_of(s, me, table, g_half, w_all):
    return pl.pallas_call(
        functools.partial(partial_kernel, s, table.shape[1]),
        out_shape=jax.ShapeDtypeStruct((s.groups, s.planes) + s.plane, jnp.float32),
        in_specs=[SMEM] * 2 + [VMEM] * 2,
        out_specs=VMEM,
        compiler_params=PARAMS,
        name="partial",
    )(me, table, g_half, w_all)


def sigma_kernel(s, slots, ks, me_ref, table_ref, begun, w_all, g_far, *outs):
    me = me_ref[0]
    side = me // s.half
    row = lax.broadcasted_iota(jnp.int32, (STRIP, LANES), 0)
    for at, k in enumerate(ks):

        def turn(kind, codes):
            codes = list(codes)
            first = kind * 2 * s.energies
            sums = [begun[k, first + j] for j in range(2 * s.energies)]
            sums = add_terms(s, slots, 1 - side, me ^ k, kind, table_ref, g_far, w_all, sums)
            if k == 0:
                for j, total in enumerate(sums):
                    outs[at][first + j] = total
                return tuple(codes)
            for low in range(0, 2 * s.energies, PAIR):
                pair = sums[low : low + PAIR]
                largest = functools.reduce(jnp.maximum, [jnp.abs(total) for total in pair])
                largest = jnp.maximum(jnp.max(largest, axis=0, keepdims=True), TINY)
                code = jnp.ceil(jnp.log2(largest) * FINE)
                inverse = jnp.exp2(code * (-1.0 / FINE)) * STEPS
                where = (first + low) // PAIR
                for i in range(s.scale_strips):
                    codes[i] = jnp.where(row + i * STRIP == where, code, codes[i])
                for j, total in enumerate(pair):
                    coded = jnp.round(total * inverse).astype(jnp.int32)
                    for i in range(s.strips):
                        strip = coded[i * STRIP : (i + 1) * STRIP].astype(jnp.int16)
                        outs[at][(first + low + j) * s.strips + i] = strip
            return tuple(codes)

        codes = lax.fori_loop(0, 2, turn, tuple(jnp.zeros((STRIP, LANES), jnp.float32) for _ in range(s.scale_strips)))
        if k != 0:
            for j in range(s.scale_strips):
                outs[at][s.planes * s.strips + j] = codes[j].astype(jnp.int32).astype(jnp.int16)


def sigma_of(s, me, table, begun, w_all, g_far, ks):
    own = jax.ShapeDtypeStruct((s.planes,) + s.plane, jnp.float32)
    coded = jax.ShapeDtypeStruct((s.planes * s.strips + s.scale_strips, STRIP, LANES), jnp.int16)
    return pl.pallas_call(
        functools.partial(sigma_kernel, s, table.shape[1], ks),
        out_shape=[own if k == 0 else coded for k in ks],
        in_specs=[SMEM] * 2 + [VMEM] * 3,
        out_specs=[VMEM] * len(ks),
        compiler_params=PARAMS,
        name="sigma",
    )(me, table, begun, w_all, g_far)


def unpack_kernel(s, order, me_ref, *refs):
    at = dict(zip(order, refs))
    blocks = [at[k] for k in range(s.groups)]
    whole_hbm, whole_ref, scales, sems = refs[s.groups :]
    me = me_ref[0]
    places = []
    for k, block in enumerate(blocks):
        cell, part, lanes = s.where(me ^ k)
        rows = slice(None) if s.parts == 1 else pl.ds(pl.multiple_of(part * s.plane[0], s.plane[0]), s.plane[0])
        places.append((cell, rows, lanes))
        if k != 0:
            for j in range(s.scale_strips):
                code = block[s.planes * s.strips + j].astype(jnp.int32).astype(jnp.float32)
                scales[k, j * STRIP : (j + 1) * STRIP] = jnp.exp2(code * (1.0 / FINE)) * (1.0 / STEPS)
    leaving = []
    for comp in range(s.comps):
        chunk = pl.ds(comp * s.energies, s.energies)
        for plane in range(comp * s.energies, (comp + 1) * s.energies):
            pair = plane // PAIR
            for k, (cell, rows, lanes) in enumerate(places):
                if k == 0:
                    value = blocks[0][plane]
                else:
                    strips = [blocks[k][plane * s.strips + i].astype(jnp.int32) for i in range(s.strips)]
                    value = jnp.concatenate(strips, axis=0).astype(jnp.float32) * scales[k, pair : pair + 1]
                whole_ref[plane, cell, rows, lanes] = value
        leaving.append(pltpu.make_async_copy(whole_ref.at[chunk], whole_hbm.at[chunk], sems.at[comp]))
        leaving[-1].start()
    for copy in leaving:
        copy.wait()


def unpack(s, me, blocks, order):
    shape = (s.planes, s.per_cell, s.rows, s.width)
    return pl.pallas_call(
        functools.partial(unpack_kernel, s, order),
        out_shape=jax.ShapeDtypeStruct(shape, jnp.float32),
        in_specs=[SMEM] + [VMEM] * s.groups,
        out_specs=ANY,
        scratch_shapes=[
            pltpu.VMEM(shape, jnp.float32),
            pltpu.VMEM((s.groups, s.scale_strips * STRIP, LANES), jnp.float32),
            pltpu.SemaphoreType.DMA((s.comps,)),
        ],
        compiler_params=PARAMS,
        name="unpack",
    )(me, *[blocks[k] for k in order])


def swap(s, block, k):
    return block if k == 0 else lax.ppermute(block, "energy", [(i, i ^ k) for i in range(s.groups)])


def send_screened(s, cell_map, screened):
    if s.parts == 1:
        return lax.all_to_all(pick_screened(s, cell_map, screened), ("energy", "cell"), 0, 0, tiled=True)
    chosen = jnp.take(screened, cell_map, axis=2).reshape(s.planes, s.cells, s.per_cell, s.held, s.width)
    whole = lax.all_to_all(chosen, "cell", 1, 3, tiled=True)
    cut = whole.reshape(s.planes, s.per_cell, s.parts, s.plane[0], s.tiles, LANES)
    cut = jnp.transpose(cut, (1, 4, 2, 0, 3, 5)).reshape((s.groups, s.planes) + s.plane)
    return lax.all_to_all(cut, "energy", 0, 0, tiled=True)


def per_device(green, screened, cell_map, shift_table, shift_count):
    s = Sizes(green, screened, lax.axis_size("energy"), lax.axis_size("cell"))
    me = lax.axis_index("energy").astype(jnp.int32).reshape(1)
    half = s.groups // 2
    far, near = list(range(half, s.groups)), list(range(half))

    screens = send_screened(s, cell_map, screened)
    greens = [swap(s, block, k) for k, block in enumerate(cut_green(s, me, green))]
    slots = jnp.arange(shift_table.shape[2], dtype=jnp.int32)
    table = jnp.where(slots < shift_count[:, :, None], jnp.clip(shift_table, 0, s.energies - 1), -1)
    table = table.reshape(s.groups * s.groups, shift_table.shape[2])
    g_near, w_all = stage_near(s, me, screens, greens[:half])
    begun = partial_of(s, me, table, g_near, w_all)
    g_far = stage_far(s, me, greens[half:], begun)
    first, later = far[2:], [0] + near[2:3] + near[3:] + near[1:2] + far[:1] + far[1:2]
    sums = {}
    for ks in (first, later):
        for k, block in zip(ks, sigma_of(s, me, table, begun, w_all, g_far, ks)):
            sums[k] = swap(s, block, k)
    return unpack(s, me, sums, later + first).reshape(green.shape)


def solution(mesh):
    placed = (
        P(None, "energy", "cell", None, None),
        P(None, "energy", None, "cell", None),
        P(),
        P(),
        P(),
    )
    return jax.shard_map(
        per_device,
        mesh=mesh,
        in_specs=placed,
        out_specs=P(None, "energy", "cell", None, None),
        check_vma=False,
    )
```
